1024 devices in a mesh: dp: 16 (over z, core), expert: 64 (over x, y).
Axes of the slice: x: 8, y: 8, z: 8, core: 2. Of those that a mesh axis runs over, the one named last changes fastest.
Arguments:
- tokens: bfloat16 [32768, 1024], P(('dp', 'expert')), may hold values from -6 to 6
- cotangent: bfloat16 [32768, 1024], P(('dp', 'expert')), may hold values from -0.59765625 to 0.59765625
- route_weight: float32 [32768, 8], P(('dp', 'expert')), may hold values from 0.1 to 1
- routed_experts: int32 [32768, 8], P(('dp', 'expert')), may hold values from 0 to 63, as said below
- gate_weights: bfloat16 [64, 1024, 384], P('expert'), may hold values from -0.1875 to 0.1875
- up_weights: bfloat16 [64, 1024, 384], P('expert'), may hold values from -0.1875 to 0.1875
- down_weights: bfloat16 [64, 384, 1024], P('expert'), may hold values from -0.3125 to 0.3125
Outputs:
- layer_out: bfloat16 [32768, 1024], P(('dp', 'expert'))
- route_gradient: float32 [32768, 8], P(('dp', 'expert'))
- gate_gradient: float32 [64, 1024, 384], P('expert', 'dp')
- up_gradient: float32 [64, 1024, 384], P('expert', 'dp')
- down_gradient: float32 [64, 384, 1024], P('expert', 'dp')
The draws below stay inside these ranges and needn't reach their ends.
Inputs may be any that keep to these rules, and one draw needn't show every extreme that they name: `routed_experts`: each row names 8 different experts. One expert is named by every row. In each aligned block of 32 rows (the rows of one device), every other expert is named by at most 4 rows, and one expert, the same in all blocks, by exactly 4 rows.
All inputs are finite; a program needn't handle non-finite values.
Results may differ from the reference program's by a relative error of at most 0.02.
Values may be sent and summed in bfloat16 or wider, within the bound.
No kernel may reach another device: no remote copies, remote signals or barrier semaphores. Data moves between devices by JAX's collectives and lax.ppermute only.
A program may use at most 32 MiB of HBM per device.

```python
import jax
import jax.numpy as jnp
from jax import lax

D = 1024
F = 384
TOP = 8
TOK_DEV = 32
EXPERTS = 64
SHARD = 2048
TOKENS = 32768
COPIES = 64
CAP_OWN = 4
CAP_HOT = 1
N_DP = 16
N_EXPERT = 64


def draw_routed_experts(key, part):
    key = jax.random.fold_in(key, 11)
    blocks = TOKENS // TOK_DEV
    others = EXPERTS - 1
    hot_key, lead_key, perm_key, roll_key = jax.random.split(key, 4)
    busiest = jax.random.randint(hot_key, (), 0, EXPERTS).astype(jnp.int32)
    colder = (busiest + 1 + jnp.arange(others, dtype=jnp.int32)) % EXPERTS
    lead = jax.random.randint(lead_key, (), 0, others).astype(jnp.int32)
    rest_pos = jnp.arange(others - 1, dtype=jnp.int32)
    rest_pos = rest_pos + (rest_pos >= lead).astype(jnp.int32)
    rest = colder[rest_pos]
    orders = jax.vmap(lambda inner: jax.random.permutation(inner, others - 1))(jax.random.split(perm_key, blocks))
    cycles = jnp.concatenate([jnp.broadcast_to(colder[lead], (blocks, 1)), rest[orders]], axis=1)
    offsets = (jnp.arange(TOK_DEV, dtype=jnp.int32)[:, None] * (TOP - 1) + jnp.arange(TOP - 1, dtype=jnp.int32)[None, :]) % others
    picked = cycles[:, offsets]
    full = jnp.concatenate([jnp.broadcast_to(busiest, (blocks, TOK_DEV, 1)), picked], axis=2)
    shifts = jax.random.randint(roll_key, (blocks, TOK_DEV, 1), 0, TOP).astype(jnp.int32)
    order = (jnp.arange(TOP, dtype=jnp.int32)[None, None, :] + shifts) % TOP
    result = jnp.take_along_axis(full, order, axis=2)
    return result.reshape(TOKENS, TOP).astype(jnp.int32)


def block_scale(rng, shape, cuts, smallest, top_value):
    gain = 1.0
    for axis_at, parts in cuts:
        heights = jax.random.uniform(jax.random.fold_in(jax.random.fold_in(rng, 6), axis_at), (parts,), jnp.float32, smallest / len(cuts), top_value / len(cuts))
        gain = gain * jnp.repeat(jnp.exp(heights), shape[axis_at] // parts).reshape((-1,) + (1,) * (len(shape) - 1 - axis_at))
    return gain


def scatter_about(own_key, dims, scale, most, pieces=(), held_as=jnp.bfloat16):
    drawn = scale * jax.random.normal(own_key, dims, jnp.float32)
    if pieces:
        drawn = drawn * block_scale(own_key, dims, pieces, -0.22, 0.18)
    return jnp.clip(drawn, -most, most).astype(held_as)


def setup_inputs(seed: int = 0) -> dict:
    keys = jax.random.split(jax.random.key(seed), 8)
    return {
        "tokens": scatter_about(keys[0], (TOKENS, D), 1.0, 6.0, ((0, 1024),)),
        "cotangent": scatter_about(keys[1], (TOKENS, D), 0.1, 0.59765625, ((0, 1024),)),
        "route_weight": jnp.clip(0.1 + 0.9 * jax.random.uniform(keys[2], (TOKENS, TOP), jnp.float32) ** block_scale(keys[2], (TOKENS, TOP), ((0, 1024),), -0.2, 0.2), 0.1, 1.0),
        "routed_experts": draw_routed_experts(jax.random.fold_in(keys[7], 71), 0),
        "gate_weights": scatter_about(keys[4], (EXPERTS, D, F), D ** -0.5, 0.1875, ((0, 64),)),
        "up_weights": scatter_about(keys[5], (EXPERTS, D, F), D ** -0.5, 0.1875, ((0, 64),)),
        "down_weights": scatter_about(keys[6], (EXPERTS, F, D), F ** -0.5, 0.3125, ((0, 64),)),
    }


highest = lax.Precision.HIGHEST


def rounded(value):
    return lax.optimization_barrier(value.astype(jnp.bfloat16)).astype(jnp.float32)


def expert_math(slot_rows, gate_weight, up_weight, down_weight):
    inputs = slot_rows[:, :, :D].astype(jnp.float32)
    scaled = slot_rows[:, :, D:].astype(jnp.float32)
    gate_value = jnp.einsum("bcd,bdf->bcf", inputs, gate_weight.astype(jnp.float32), precision=highest)
    up_value = jnp.einsum("bcd,bdf->bcf", inputs, up_weight.astype(jnp.float32), precision=highest)
    sigmoid = jax.nn.sigmoid(gate_value)
    active = gate_value * sigmoid
    hidden = rounded(active * up_value)
    output = jnp.einsum("bcf,bfd->bcd", hidden, down_weight.astype(jnp.float32), precision=highest).astype(jnp.bfloat16)
    upstream = jnp.einsum("bcd,bfd->bcf", scaled, down_weight.astype(jnp.float32), precision=highest)
    slope_term = sigmoid * (1.0 + gate_value * (1.0 - sigmoid))
    gate_delta = rounded(upstream * up_value * slope_term)
    up_delta = rounded(upstream * active)
    grad_gate = jnp.einsum("bcd,bcf->bdf", inputs, gate_delta, precision=highest)
    grad_up = jnp.einsum("bcd,bcf->bdf", inputs, up_delta, precision=highest)
    grad_down = jnp.einsum("bcf,bcd->bfd", hidden, scaled, precision=highest)
    return output, rounded(grad_gate), rounded(grad_up), rounded(grad_down)


def reference(tokens, cotangent, route_weight, routed_experts, gate_weights, up_weights, down_weights):
    expert_range = jnp.arange(EXPERTS, dtype=jnp.int32)
    totals_all = jnp.sum((routed_experts.reshape(-1)[:, None] == expert_range[None, :]).astype(jnp.int32), axis=0)
    busiest = jnp.argmax(totals_all).astype(jnp.int32)
    own_cap = N_EXPERT * CAP_OWN
    hot_cap = N_EXPERT * CAP_HOT
    route_count = SHARD * TOP
    route_token = jnp.arange(route_count, dtype=jnp.int32) // TOP
    local_row = route_token % TOK_DEV
    source = route_token // TOK_DEV
    copy_rank = route_token % COPIES
    hot_gate = jnp.broadcast_to(gate_weights[busiest][None], (COPIES, D, F))
    hot_up = jnp.broadcast_to(up_weights[busiest][None], (COPIES, D, F))
    hot_down = jnp.broadcast_to(down_weights[busiest][None], (COPIES, F, D))

    def one_group(totals, shard_data):
        shard_tokens, shard_cotangent, shard_weights, shard_experts = shard_data
        flat_experts = shard_experts.reshape(route_count)
        flat_weights = shard_weights.reshape(route_count)
        is_hot = flat_experts == busiest
        counts_table = (flat_experts[:, None] == expert_range[None, :]).astype(jnp.int32)
        counts_table = counts_table * (1 - is_hot.astype(jnp.int32))[:, None]
        cold_rank = jnp.sum((jnp.cumsum(counts_table, axis=0) - counts_table) * counts_table, axis=1)
        own_index = jnp.where(is_hot, EXPERTS * own_cap, flat_experts * own_cap + cold_rank).astype(jnp.int32)
        hot_index = jnp.where(is_hot, copy_rank * hot_cap + source * CAP_HOT + local_row // COPIES, COPIES * hot_cap).astype(jnp.int32)
        route_tokens = shard_tokens[route_token]
        route_cot = shard_cotangent[route_token].astype(jnp.float32)
        route_scaled = (flat_weights[:, None] * route_cot).astype(jnp.bfloat16)
        route_rows = jnp.concatenate([route_tokens, route_scaled], axis=1)
        own_rows = jnp.zeros((EXPERTS * own_cap, 2 * D), jnp.bfloat16).at[own_index].set(route_rows, mode="drop")
        hot_rows = jnp.zeros((COPIES * hot_cap, 2 * D), jnp.bfloat16).at[hot_index].set(route_rows, mode="drop")
        own_out, own_gate, own_up, own_down = expert_math(own_rows.reshape(EXPERTS, own_cap, 2 * D), gate_weights, up_weights, down_weights)
        hot_out, hot_gate_part, hot_up_part, hot_down_part = expert_math(hot_rows.reshape(COPIES, hot_cap, 2 * D), hot_gate, hot_up, hot_down)
        own_flat = own_out.reshape(EXPERTS * own_cap, D)
        hot_flat = hot_out.reshape(COPIES * hot_cap, D)
        route_out = jnp.where(is_hot[:, None], jnp.take(hot_flat, hot_index, axis=0, mode="clip"), jnp.take(own_flat, own_index, axis=0, mode="clip"))
        route_values = lax.optimization_barrier(route_out).astype(jnp.float32)
        layer_block = jnp.sum((flat_weights[:, None] * route_values).reshape(SHARD, TOP, D), axis=1).astype(jnp.bfloat16)
        gradient_block = jnp.sum(route_values * route_cot, axis=1).reshape(SHARD, TOP)
        totals = (totals[0] + own_gate, totals[1] + own_up, totals[2] + own_down,
                  totals[3] + jnp.sum(hot_gate_part, axis=0), totals[4] + jnp.sum(hot_up_part, axis=0), totals[5] + jnp.sum(hot_down_part, axis=0))
        return totals, (layer_block, gradient_block)

    start = (jnp.zeros((EXPERTS, D, F), jnp.float32), jnp.zeros((EXPERTS, D, F), jnp.float32), jnp.zeros((EXPERTS, F, D), jnp.float32),
             jnp.zeros((D, F), jnp.float32), jnp.zeros((D, F), jnp.float32), jnp.zeros((F, D), jnp.float32))
    stacked = (tokens.reshape(N_DP, SHARD, D), cotangent.reshape(N_DP, SHARD, D),
               route_weight.reshape(N_DP, SHARD, TOP), routed_experts.reshape(N_DP, SHARD, TOP))
    totals, blocks = lax.scan(one_group, start, stacked)
    layer_out = blocks[0].reshape(TOKENS, D)
    route_gradient = blocks[1].reshape(TOKENS, TOP)
    gate_gradient = totals[0].at[busiest].add(totals[3])
    up_gradient = totals[1].at[busiest].add(totals[4])
    down_gradient = totals[2].at[busiest].add(totals[5])
    return (layer_out, route_gradient, gate_gradient, up_gradient, down_gradient)
```

```python
import jax
import jax.numpy as jnp
import numpy as np
from jax import lax
from jax.sharding import PartitionSpec as P

f32 = jnp.float32
bf16 = jnp.bfloat16
highest = lax.Precision.HIGHEST


def dot(lhs, rhs, lhs_dim, rhs_dim, precision=None):
    dims = (((lhs_dim,), (rhs_dim,)), ((), ()))
    return lax.dot_general(lhs, rhs, dims, precision=precision, preferred_element_type=f32)


def plane_exchange(blocks):
    return lax.all_to_all(blocks, "expert", split_axis=0, concat_axis=0, tiled=True)


def core_swap(block):
    size = lax.axis_size("dp")
    return lax.ppermute(block, "dp", [(i, i ^ 1) for i in range(size)])


def z_exchange(blocks):
    size = lax.axis_size("dp")
    groups = [list(range(core, size, 2)) for core in range(2)]
    return lax.all_to_all(
        blocks, "dp", split_axis=0, concat_axis=0, tiled=True, axis_index_groups=groups
    )


def pad_blocks(blocks, count):
    return jnp.pad(blocks, ((0, count - blocks.shape[0]),) + ((0, 0),) * (blocks.ndim - 1))


def deltas(gate_value, up_value, upstream):
    sigmoid = jax.nn.sigmoid(gate_value)
    active = gate_value * sigmoid
    hidden = (active * up_value).astype(bf16)
    gate_delta = (upstream * up_value * (sigmoid * (1.0 + gate_value * (1.0 - sigmoid)))).astype(bf16)
    up_delta = (upstream * active).astype(bf16)
    return hidden, gate_delta, up_delta


def routing(routed, weight, experts):
    rows = routed.shape[1]
    names = jnp.arange(experts, dtype=jnp.int32)
    hits = routed[None] == names[:, None, None]
    named = jnp.any(hits, axis=1)
    busiest = jnp.argmax(jnp.sum(named.astype(jnp.int32), axis=1)).astype(jnp.int32)
    table = jnp.sum(jnp.where(hits, weight[None], 0.0), axis=1)
    cold = named & (names != busiest)[:, None]
    before = jnp.arange(rows)[:, None] < jnp.arange(rows)[None, :]
    rank = dot(cold.astype(bf16), before.astype(bf16), 1, 0).astype(jnp.int32)
    slot = jnp.arange(8, dtype=jnp.int32) % 4
    place = cold[:, None, :] & (rank[:, None, :] == slot[None, :, None])
    return busiest, hits, table, place


def own_expert(arrived, gate, up, down):
    experts, _, features = arrived.shape
    hidden_units = gate.shape[1]
    rows = experts * 4
    inputs = arrived[:, :4].reshape(rows, features)
    scaled = arrived[:, 4:].reshape(rows, features)
    gate_value = dot(inputs, gate, 1, 0)
    up_value = dot(inputs, up, 1, 0)
    upstream = dot(scaled, down, 1, 1)
    hidden, gate_delta, up_delta = deltas(gate_value, up_value, upstream)
    output = dot(hidden, down, 1, 0).astype(bf16)
    output = output.reshape(experts, 4, 2, features // 2).transpose(0, 2, 1, 3)
    output = output.reshape(experts, 8, features // 2)
    size = lax.axis_size("dp")

    def stripes(matrix):
        height, width = matrix.shape
        striped = matrix.astype(bf16).reshape(size, height // size, width // 128, 128)
        return striped.transpose(0, 2, 1, 3).reshape(size, -1, 128)

    partial = jnp.concatenate(
        [
            stripes(dot(inputs, gate_delta, 0, 0)),
            stripes(dot(inputs, up_delta, 0, 0)),
            stripes(dot(hidden, scaled, 0, 0)),
        ],
        axis=1,
    )
    return output, partial


def hot_expert(gathered, sliced, core):
    features = sliced.shape[1]
    units = sliced.shape[0] // 3
    inputs = gathered[:, :features]
    scaled = gathered[:, features:]
    both = dot(sliced[: 2 * units], inputs, 1, 1)
    upstream = dot(sliced[2 * units :], scaled, 1, 1)
    hidden, gate_delta, up_delta = deltas(both[:units], both[units:], upstream)
    output = dot(hidden, sliced[2 * units :], 0, 0).astype(bf16)
    pair = jnp.concatenate([gate_delta, up_delta], axis=0)
    empty = jnp.zeros_like(pair)
    spread = jnp.concatenate(
        [
            jnp.where(core == 0, pair, empty),
            jnp.where(core == 1, pair, empty),
            jnp.zeros((128 - 4 * units, pair.shape[1]), bf16),
        ],
        axis=0,
    )
    pair_gradient = dot(inputs, spread, 0, 1).astype(bf16)
    down_gradient = dot(hidden, scaled, 1, 0).astype(bf16)
    return output, pair_gradient, down_gradient


def on_device(
    tokens, cotangent, route_weight, routed_experts, gate_weights, up_weights, down_weights
):
    experts = lax.axis_size("expert")
    size = lax.axis_size("dp")
    depth = size // 2
    mine = lax.axis_index("expert")
    shard = lax.axis_index("dp")
    core = shard % 2
    rows, features = tokens.shape
    half = features // 2
    gate, up, down = gate_weights[0], up_weights[0], down_weights[0]
    width = gate.shape[1]
    units = width // size

    busiest, hits, table, place = routing(routed_experts.T, route_weight.T, experts)
    hot_weight = lax.dynamic_index_in_dim(table, busiest, 0, keepdims=False)
    wide_cotangent = cotangent.astype(f32)
    hot_scaled = (hot_weight[:, None] * wide_cotangent).astype(bf16)
    gathered = lax.all_gather(
        jnp.concatenate([tokens, hot_scaled], axis=1), "dp", axis=0, tiled=True
    )

    is_token = (jnp.arange(8) < 4)[None, :, None]
    picks = jnp.concatenate([place & is_token, place & ~is_token], axis=2)
    slot_weight = jnp.sum(jnp.where(place, table[:, None, :], 0.0), axis=2)
    factor = jnp.where(jnp.arange(8)[None, :] < 4, 1.0, slot_weight).reshape(experts * 8, 1)
    stacked = jnp.concatenate([tokens, cotangent], axis=0)
    picked = dot(picks.astype(bf16).reshape(experts * 8, 2 * rows), stacked, 1, 0)
    outgoing = (picked * factor).astype(bf16).reshape(experts, 8, features)

    unit = shard * units + jnp.arange(units, dtype=jnp.int32)
    choose = (jnp.arange(width, dtype=jnp.int32)[None, :] == unit[:, None]).astype(bf16)
    pieces = jnp.concatenate(
        [dot(choose, gate, 1, 1), dot(choose, up, 1, 1), dot(choose, down, 1, 0)], axis=0
    ).astype(bf16)
    bands, spans = 3 * units // 8, features // 256
    pieces = pieces.reshape(bands, 8, spans, 256).transpose(0, 2, 1, 3)
    pieces = pad_blocks(pieces.reshape(bands * spans, 8, 256), experts)

    arrived = plane_exchange(jnp.concatenate([outgoing, pieces], axis=2))
    piece = lax.dynamic_index_in_dim(arrived[:, :, features:], busiest, 0, keepdims=True)
    sliced = plane_exchange(jnp.broadcast_to(piece, (experts, 8, 256)))
    sliced = sliced[: bands * spans].reshape(bands, spans, 8, 256).transpose(0, 2, 1, 3)
    sliced = sliced.reshape(3 * units, features)

    returning, partial = own_expert(arrived[:, :, :features], gate, up, down)
    own_sum = lax.psum_scatter(partial, "dp", scatter_dimension=0, tiled=True)[0].astype(f32)

    hot_part, pair_gradient, hot_down = hot_expert(gathered, sliced, core)
    strip = features // size
    pair_blocks = pair_gradient.reshape(depth, 2, 2, strip // 2, 128).transpose(0, 1, 3, 2, 4)
    both = jnp.concatenate(
        [
            hot_part.reshape(depth, 2, rows, features),
            pair_blocks.reshape(depth, 2, rows, 256),
        ],
        axis=3,
    )
    kept = jnp.where(core == 0, both[:, 0], both[:, 1])
    passed = jnp.where(core == 0, both[:, 1], both[:, 0])
    joined = (kept.astype(f32) + core_swap(passed).astype(f32)).astype(bf16)
    joined = z_exchange(joined)
    hot_out = jnp.sum(joined[:, :, :features].astype(f32), axis=0).astype(bf16)
    pair_tiles = joined[:, :, features:].reshape(depth, 4, 8, 2, 128).transpose(0, 3, 1, 2, 4)
    pair_tiles = pad_blocks(pair_tiles.reshape(depth * 8, 8, 128), experts)
    down_tiles = hot_down.reshape(units // 8, 8, features // 128, 128).transpose(0, 2, 1, 3)
    down_tiles = down_tiles.reshape(-1, 8, 128)
    down_count = down_tiles.shape[0]
    down_tiles = pad_blocks(down_tiles, experts)

    back = plane_exchange(jnp.concatenate([returning, pair_tiles, down_tiles], axis=2))
    hot_piece = jnp.sum(back[:, :, half:].astype(f32), axis=0).astype(bf16)
    hot_blocks = plane_exchange(jnp.broadcast_to(hot_piece[None], (experts, 8, 256)))

    results = back[:, :, :half].reshape(experts * 8, half)
    weighting = jnp.where(place, table[:, None, :], 0.0)
    halves = jnp.concatenate(
        [jnp.where(is_token, weighting, 0.0), jnp.where(is_token, 0.0, weighting)], axis=2
    ).reshape(experts * 8, 2 * rows)
    summed = dot(halves, results.astype(f32), 0, 0, highest)
    wide_hot = hot_out.astype(f32)
    layer_out = jnp.concatenate([summed[:rows], summed[rows:]], axis=1)
    layer_out = (layer_out + hot_weight[:, None] * wide_hot).astype(bf16)

    products = jnp.where(
        is_token,
        dot(results, cotangent[:, :half], 1, 1).reshape(experts, 8, rows),
        dot(results, cotangent[:, half:], 1, 1).reshape(experts, 8, rows),
    )
    by_expert = jnp.sum(jnp.where(place, products, 0.0), axis=1)
    hot_product = jnp.sum(wide_hot * wide_cotangent, axis=1)
    is_busiest = jnp.arange(experts, dtype=jnp.int32)[:, None] == busiest
    by_expert = by_expert + jnp.where(is_busiest, hot_product[None], 0.0)
    route_gradient = jnp.sum(jnp.where(hits, by_expert[:, None, :], 0.0), axis=0).T

    lane = np.arange(depth * 128)
    within = lane % 128
    column = (within % (2 * units)) // units * width
    column = column + (lane // 128 * 2 + within // (2 * units)) * units + within % units
    column = np.where(within < 4 * units, column, -1).astype(np.int32)
    spread = (jnp.asarray(column)[:, None] == jnp.arange(2 * width, dtype=jnp.int32)).astype(bf16)
    hot_pair = hot_blocks[: depth * 8, :, :128].reshape(depth, strip, 128).transpose(1, 0, 2)
    hot_pair = dot(hot_pair.reshape(strip, depth * 128), spread, 1, 0)
    hot_down = hot_blocks[:down_count, :, 128:].reshape(units // 8, features // 128, 8, 128)
    hot_down = hot_down.transpose(0, 2, 1, 3).reshape(units, features).astype(f32)

    def unstripe(block, height):
        return block.reshape(-1, height, 128).transpose(1, 0, 2).reshape(height, -1)

    count = strip * width // 128
    home = mine == busiest
    gate_gradient = unstripe(own_sum[:count], strip) + jnp.where(home, hot_pair[:, :width], 0.0)
    up_gradient = unstripe(own_sum[count : 2 * count], strip) + jnp.where(
        home, hot_pair[:, width:], 0.0
    )
    down_gradient = unstripe(own_sum[2 * count :], units) + jnp.where(home, hot_down, 0.0)
    return (layer_out, route_gradient, gate_gradient[None], up_gradient[None], down_gradient[None])


def solution(mesh):
    in_specs = (
        P(("dp", "expert"), None),
        P(("dp", "expert"), None),
        P(("dp", "expert"), None),
        P(("dp", "expert"), None),
        P("expert", None, None),
        P("expert", None, None),
        P("expert", None, None),
    )
    out_specs = (
        P(("dp", "expert"), None),
        P(("dp", "expert"), None),
        P("expert", "dp", None),
        P("expert", "dp", None),
        P("expert", "dp", None),
    )
    return jax.shard_map(
        on_device, mesh=mesh, in_specs=in_specs, out_specs=out_specs, check_vma=False
    )
```

```python
import functools

import jax
import jax.numpy as jnp
from jax import lax
from jax.experimental import pallas as pl
from jax.experimental.pallas import tpu as pltpu
from jax.sharding import PartitionSpec as P

f32 = jnp.float32
bf16 = jnp.bfloat16
highest = lax.Precision.HIGHEST


def dot(lhs, rhs, lhs_dim, rhs_dim, precision=None):
    dims = (((lhs_dim,), (rhs_dim,)), ((), ()))
    return lax.dot_general(lhs, rhs, dims, precision=precision, preferred_element_type=f32)


def plane_exchange(blocks):
    return lax.all_to_all(blocks, "expert", split_axis=0, concat_axis=0, tiled=True)


def core_swap(block):
    size = lax.axis_size("dp")
    return lax.ppermute(block, "dp", [(i, i ^ 1) for i in range(size)])


def z_exchange(blocks):
    size = lax.axis_size("dp")
    groups = [list(range(core, size, 2)) for core in range(2)]
    return lax.all_to_all(
        blocks, "dp", split_axis=0, concat_axis=0, tiled=True, axis_index_groups=groups
    )


def z_reduce_scatter(blocks):
    size = lax.axis_size("dp")
    groups = [list(range(core, size, 2)) for core in range(2)]
    return lax.psum_scatter(
        blocks, "dp", scatter_dimension=0, tiled=True, axis_index_groups=groups
    )


def add(one, other):
    return (one.astype(f32) + other.astype(f32)).astype(bf16)


def pad_blocks(blocks, count):
    return jnp.pad(blocks, ((0, count - blocks.shape[0]),) + ((0, 0),) * (blocks.ndim - 1))


def routing(routed, weight, experts):
    rows = routed.shape[1]
    names = jnp.arange(experts, dtype=jnp.int32)
    hits = routed[None] == names[:, None, None]
    named = jnp.any(hits, axis=1)
    busiest = jnp.argmax(jnp.sum(named.astype(jnp.int32), axis=1)).astype(jnp.int32)
    table = jnp.sum(jnp.where(hits, weight[None], 0.0), axis=1)
    cold = named & (names != busiest)[:, None]
    before = jnp.arange(rows)[:, None] < jnp.arange(rows)[None, :]
    rank = dot(cold.astype(bf16), before.astype(bf16), 1, 0).astype(jnp.int32)
    slot = jnp.arange(8, dtype=jnp.int32) % 4
    place = cold[:, None, :] & (rank[:, None, :] == slot[None, :, None])
    return busiest, hits, table, place


def in_vmem(count):
    return [pl.BlockSpec(memory_space=pltpu.VMEM)] * count


def own_kernel(
    core_ref, rows_ref, gate_ref, up_ref, down_ref, out_ref, kept_ref, passed_ref, grads, down_grads
):
    features, width = gate_ref.shape
    depth = kept_ref.shape[0]
    half = features // 2
    strip = features // (2 * depth)
    units = width // (2 * depth)
    lanes = width // 128
    core = core_ref[0]
    sides = ((kept_ref, core), (passed_ref, 1 - core))
    rows = rows_ref[:, :features]
    down = down_ref[...]
    gate_value = dot(rows, gate_ref[...], 1, 0)
    up_value = dot(rows, up_ref[...], 1, 0)
    upstream = dot(rows, down, 1, 1)
    count = gate_value.shape[0]
    upstream = pltpu.roll(upstream, count - 4, 0)
    sigmoid = jax.nn.sigmoid(gate_value)
    active = gate_value * sigmoid
    slope = sigmoid * (1.0 + gate_value * (1.0 - sigmoid))
    is_token = lax.broadcasted_iota(jnp.int32, (count, width), 0) % 8 < 4
    hidden = jnp.where(is_token, active * up_value, 0.0)
    shifted = pltpu.roll(hidden, 4, 0).astype(bf16)
    hidden = hidden.astype(bf16)
    gate_delta = jnp.where(is_token, upstream * up_value * slope, 0.0).astype(bf16)
    up_delta = jnp.where(is_token, upstream * active, 0.0).astype(bf16)
    for index, delta in enumerate((gate_delta, up_delta)):
        grads[...] = dot(rows, delta, 0, 0)
        for z in range(depth):
            for ref, side in sides:
                start = pl.multiple_of((2 * z + side) * strip, strip)
                block = grads[pl.ds(start, strip), :].astype(bf16)
                for lane in range(lanes):
                    at = (index * lanes + lane) * strip
                    ref[z, at : at + strip, :] = block[:, lane * 128 : lane * 128 + 128]
    down_grads[...] = dot(shifted, rows, 0, 0)
    base = 2 * lanes * strip
    for z in range(depth):
        for ref, side in sides:
            start = pl.multiple_of((2 * z + side) * units, 8)
            block = down_grads[pl.ds(start, units), :]
            for lane in range(0, features // 128, 2):
                at = base + lane * units
                pair = [block[:, i * 128 : i * 128 + 128] for i in (lane, lane + 1)]
                ref[z, at : at + 2 * units, :] = jnp.concatenate(pair, axis=0).astype(bf16)
    output = dot(hidden, down[:, :half], 1, 0) + dot(shifted, down[:, half:], 1, 0)
    out_ref[...] = output.astype(bf16)


def own_expert(core, rows, gate, up, down, depth):
    features, width = gate.shape
    side = jax.ShapeDtypeStruct((depth, 3 * features * width // (2 * depth) // 128, 128), bf16)
    return pl.pallas_call(
        own_kernel,
        out_shape=(jax.ShapeDtypeStruct((rows.shape[0], features // 2), bf16), side, side),
        in_specs=[pl.BlockSpec(memory_space=pltpu.SMEM)] + in_vmem(4),
        out_specs=tuple(in_vmem(3)),
        scratch_shapes=[pltpu.VMEM((features, width), f32), pltpu.VMEM((width, features), f32)],
        compiler_params=pltpu.CompilerParams(vmem_limit_bytes=48 * 2**20),
    )(core, rows, gate, up, down)


def hot_kernel(units, core_ref, rows_ref, blocks_ref, kept_ref, passed_ref, grads_ref, part):
    features = part.shape[1]
    depth = kept_ref.shape[0]
    group = part.shape[0] // (2 * depth)
    spans = features // 256
    height = -(-3 * units // 16) * 16
    core = core_ref[0]
    inputs = rows_ref[:, :features]
    scaled = rows_ref[:, features:]
    sliced = jnp.concatenate(
        [blocks_ref[span * height : span * height + height, :] for span in range(spans)], axis=1
    )
    down = sliced[2 * units :]
    both = dot(sliced[: 2 * units], inputs, 1, 1)
    upstream = dot(down, scaled, 1, 1)[:units]
    gate_value, up_value = both[:units], both[units:]
    sigmoid = jax.nn.sigmoid(gate_value)
    active = gate_value * sigmoid
    slope = sigmoid * (1.0 + gate_value * (1.0 - sigmoid))
    pair = jnp.concatenate([upstream * up_value * slope, upstream * active], axis=0).astype(bf16)
    spare = jnp.zeros((height - 3 * units, gate_value.shape[1]), f32)
    hidden = active * up_value
    if spare.shape[0]:
        hidden = jnp.concatenate([hidden, spare], axis=0)
    hidden = hidden.astype(bf16)
    part[...] = dot(hidden, down, 0, 0)
    for z in range(depth):
        for ref, side in ((kept_ref, core), (passed_ref, 1 - core)):
            start = pl.multiple_of((2 * z + side) * group, group)
            block = part[pl.ds(start, group), :].astype(bf16)
            for lane in range(features // 128):
                ref[z, lane * group : lane * group + group, :] = block[
                    :, lane * 128 : lane * 128 + 128
                ]
    grads = jnp.concatenate([dot(pair, inputs, 1, 0), dot(hidden, scaled, 1, 0)], axis=0)
    grads = grads.astype(bf16)
    for span in range(spans):
        grads_ref[span * height : span * height + height, :] = grads[
            :, span * 256 : span * 256 + 256
        ]
    used = spans * height
    grads_ref[used:, :] = jnp.zeros((grads_ref.shape[0] - used, 256), bf16)


def hot_expert(core, gathered, blocks, units, depth):
    total, features = gathered.shape[0], gathered.shape[1] // 2
    side = jax.ShapeDtypeStruct((depth, total // (2 * depth) * features // 128, 128), bf16)
    return pl.pallas_call(
        functools.partial(hot_kernel, units),
        out_shape=(side, side, jax.ShapeDtypeStruct(blocks.shape, bf16)),
        in_specs=[pl.BlockSpec(memory_space=pltpu.SMEM)] + in_vmem(2),
        out_specs=tuple(in_vmem(3)),
        scratch_shapes=[pltpu.VMEM((total, features), f32)],
        compiler_params=pltpu.CompilerParams(vmem_limit_bytes=48 * 2**20),
    )(core, gathered, blocks)


def on_device(
    tokens, cotangent, route_weight, routed_experts, gate_weights, up_weights, down_weights
):
    experts = lax.axis_size("expert")
    size = lax.axis_size("dp")
    depth = size // 2
    mine = lax.axis_index("expert")
    shard = lax.axis_index("dp")
    core = shard % 2
    core_word = core.astype(jnp.int32).reshape(1)
    rows, features = tokens.shape
    half = features // 2
    gate, up, down = gate_weights[0], up_weights[0], down_weights[0]
    width = gate.shape[1]
    units = width // size
    strip = features // size

    busiest, hits, table, place = routing(routed_experts.T, route_weight.T, experts)
    hot_weight = lax.dynamic_index_in_dim(table, busiest, 0, keepdims=False)
    wide_cotangent = cotangent.astype(f32)
    hot_scaled = (hot_weight[:, None] * wide_cotangent).astype(bf16)
    gathered = lax.all_gather(
        jnp.concatenate([tokens, hot_scaled], axis=1), "dp", axis=0, tiled=True
    )

    is_token = (jnp.arange(8) < 4)[None, :, None]
    picks = jnp.concatenate([place & is_token, place & ~is_token], axis=2)
    slot_weight = jnp.sum(jnp.where(place, table[:, None, :], 0.0), axis=2)
    factor = jnp.where(jnp.arange(8)[None, :] < 4, 1.0, slot_weight).reshape(experts * 8, 1)
    stacked = jnp.concatenate([tokens, cotangent], axis=0)
    picked = dot(picks.astype(bf16).reshape(experts * 8, 2 * rows), stacked, 1, 0)
    outgoing = (picked * factor).astype(bf16).reshape(experts, 8, features)

    unit = shard * units + jnp.arange(units, dtype=jnp.int32)
    choose = (jnp.arange(width, dtype=jnp.int32)[None, :] == unit[:, None]).astype(bf16)
    height, spans = -(-3 * units // 16) * 16, features // 256
    pieces = jnp.concatenate(
        [
            dot(choose, gate, 1, 1).astype(bf16),
            dot(choose, up, 1, 1).astype(bf16),
            dot(choose, down, 1, 0).astype(bf16),
            jnp.zeros((height - 3 * units, features), bf16),
        ],
        axis=0,
    )
    pieces = pieces.reshape(height // 8, 8, spans, 256).transpose(2, 0, 1, 3)
    pieces = pad_blocks(pieces.reshape(height // 8 * spans, 8, 256), experts)

    arrived = plane_exchange(jnp.concatenate([outgoing, pieces], axis=2))
    piece = lax.dynamic_index_in_dim(arrived[:, :, features:], busiest, 0, keepdims=True)
    blocks = plane_exchange(jnp.broadcast_to(piece, (experts, 8, 256)))

    returning, own_kept, own_passed = own_expert(
        core_word, arrived.reshape(experts * 8, features + 256), gate, up, down, depth
    )
    own_came = core_swap(own_passed)
    hot_kept, hot_passed, hot_grads = hot_expert(
        core_word, gathered, blocks.reshape(experts * 8, 256), units, depth
    )
    hot_came = core_swap(hot_passed)
    joined = jnp.concatenate([add(own_kept, own_came), add(hot_kept, hot_came)], axis=1)
    summed = z_reduce_scatter(joined)[0]
    own_rows = own_kept.shape[1]
    own_sum = summed[:own_rows].astype(f32)
    hot_out = summed[own_rows:].reshape(features // 128, rows, 128)
    hot_out = hot_out.transpose(1, 0, 2).reshape(rows, features)

    back = plane_exchange(
        jnp.concatenate(
            [returning.reshape(experts, 8, half), hot_grads.reshape(experts, 8, 256)], axis=2
        )
    )
    hot_piece = jnp.sum(back[:, :, half:].astype(f32), axis=0).astype(bf16)
    hot_blocks = plane_exchange(jnp.broadcast_to(hot_piece[None], (experts, 8, 256)))
    hot_rows = hot_blocks.reshape(experts * 8, 256)[: spans * height]
    hot_rows = hot_rows.reshape(spans, height, 256).transpose(1, 0, 2).reshape(height, features)
    hot_down = hot_rows[2 * units : 3 * units].astype(f32)
    pair = hot_rows[: 2 * units].reshape(2 * units, depth, 2, strip).transpose(1, 2, 0, 3)
    pair_kept = jnp.where(core == 0, pair[:, 0], pair[:, 1])
    pair_came = core_swap(jnp.where(core == 0, pair[:, 1], pair[:, 0]))
    pair = jnp.concatenate(
        [
            jnp.where(core == 0, pair_kept, pair_came),
            jnp.where(core == 0, pair_came, pair_kept),
        ],
        axis=2,
    )
    pair = z_exchange(pair).reshape(depth, 2, units, 2, strip)
    pair = pair.transpose(1, 4, 0, 3, 2).reshape(2, strip, width).astype(f32)

    results = back[:, :, :half].reshape(experts * 8, half)
    weighting = jnp.where(place, table[:, None, :], 0.0)
    halves = jnp.concatenate(
        [jnp.where(is_token, weighting, 0.0), jnp.where(is_token, 0.0, weighting)], axis=2
    ).reshape(experts * 8, 2 * rows)
    weighed = dot(halves, results.astype(f32), 0, 0, highest)
    wide_hot = hot_out.astype(f32)
    layer_out = jnp.concatenate([weighed[:rows], weighed[rows:]], axis=1)
    layer_out = (layer_out + hot_weight[:, None] * wide_hot).astype(bf16)

    products = jnp.where(
        is_token,
        dot(results, cotangent[:, :half], 1, 1).reshape(experts, 8, rows),
        dot(results, cotangent[:, half:], 1, 1).reshape(experts, 8, rows),
    )
    by_expert = jnp.sum(jnp.where(place, products, 0.0), axis=1)
    hot_product = jnp.sum(wide_hot * wide_cotangent, axis=1)
    is_busiest = jnp.arange(experts, dtype=jnp.int32)[:, None] == busiest
    by_expert = by_expert + jnp.where(is_busiest, hot_product[None], 0.0)
    route_gradient = jnp.sum(jnp.where(hits, by_expert[:, None, :], 0.0), axis=0).T

    def unstripe(block, tall):
        return block.reshape(-1, tall, 128).transpose(1, 0, 2).reshape(tall, -1)

    count = strip * width // 128
    home = mine == busiest
    gate_gradient = unstripe(own_sum[:count], strip) + jnp.where(home, pair[0], 0.0)
    up_gradient = unstripe(own_sum[count : 2 * count], strip) + jnp.where(home, pair[1], 0.0)
    down_gradient = unstripe(own_sum[2 * count :], units) + jnp.where(home, hot_down, 0.0)
    return (layer_out, route_gradient, gate_gradient[None], up_gradient[None], down_gradient[None])


def solution(mesh):
    in_specs = (
        P(("dp", "expert"), None),
        P(("dp", "expert"), None),
        P(("dp", "expert"), None),
        P(("dp", "expert"), None),
        P("expert", None, None),
        P("expert", None, None),
        P("expert", None, None),
    )
    out_specs = (
        P(("dp", "expert"), None),
        P(("dp", "expert"), None),
        P("expert", "dp", None),
        P("expert", "dp", None),
        P("expert", "dp", None),
    )
    return jax.shard_map(
        on_device, mesh=mesh, in_specs=in_specs, out_specs=out_specs, check_vma=False
    )
```

```python
import functools

import jax
import jax.numpy as jnp
import numpy as np
from jax import lax
from jax.experimental import pallas as pl
from jax.experimental.pallas import tpu as pltpu
from jax.sharding import PartitionSpec as P

f32 = jnp.float32
bf16 = jnp.bfloat16
highest = lax.Precision.HIGHEST


def dot(lhs, rhs, lhs_dim, rhs_dim, precision=None):
    dims = (((lhs_dim,), (rhs_dim,)), ((), ()))
    return lax.dot_general(lhs, rhs, dims, precision=precision, preferred_element_type=f32)


def plane_exchange(blocks):
    return lax.all_to_all(blocks, "expert", split_axis=0, concat_axis=0, tiled=True)


def core_swap(block):
    size = lax.axis_size("dp")
    return lax.ppermute(block, "dp", [(i, i ^ 1) for i in range(size)])


def z_exchange(blocks):
    size = lax.axis_size("dp")
    groups = [list(range(core, size, 2)) for core in range(2)]
    return lax.all_to_all(
        blocks, "dp", split_axis=0, concat_axis=0, tiled=True, axis_index_groups=groups
    )


def z_reduce_scatter(blocks):
    size = lax.axis_size("dp")
    groups = [list(range(core, size, 2)) for core in range(2)]
    return lax.psum_scatter(
        blocks, "dp", scatter_dimension=0, tiled=True, axis_index_groups=groups
    )


def add(one, other):
    return (one.astype(f32) + other.astype(f32)).astype(bf16)


def pad_blocks(blocks, count):
    return jnp.pad(blocks, ((0, count - blocks.shape[0]),) + ((0, 0),) * (blocks.ndim - 1))


def routing(routed, weight, experts):
    rows = routed.shape[1]
    names = jnp.arange(experts, dtype=jnp.int32)
    hits = routed[None] == names[:, None, None]
    named = jnp.any(hits, axis=1)
    busiest = jnp.argmax(jnp.sum(named.astype(jnp.int32), axis=1)).astype(jnp.int32)
    table = jnp.sum(jnp.where(hits, weight[None], 0.0), axis=1)
    cold = named & (names != busiest)[:, None]
    before = jnp.arange(rows)[:, None] < jnp.arange(rows)[None, :]
    rank = dot(cold.astype(bf16), before.astype(bf16), 1, 0).astype(jnp.int32)
    slot = jnp.arange(8, dtype=jnp.int32) % 4
    place = cold[:, None, :] & (rank[:, None, :] == slot[None, :, None])
    return busiest, hits, table, place


def in_vmem(count):
    return [pl.BlockSpec(memory_space=pltpu.VMEM)] * count


def pack_kernel(
    shard_ref, tokens_ref, cotangent_ref, weight_ref, routed_ref, gate_ref, up_ref, down_ref,
    out_ref, hot_ref, busiest_ref, size
):
    rows, features = tokens_ref.shape
    width = gate_ref.shape[1]
    units = width // size
    height, spans = -(-3 * units // 16) * 16, features // 256
    total = out_ref.shape[0]
    experts = total // 8
    names = lax.broadcasted_iota(jnp.int32, (experts, rows), 0)
    named = jnp.zeros((experts, rows), f32)
    table = jnp.zeros((experts, rows), f32)
    for k in range(routed_ref.shape[0]):
        hit = routed_ref[k : k + 1, :] == names
        named = jnp.where(hit, 1.0, named)
        table = jnp.where(hit, weight_ref[k : k + 1, :], table)
    counts = jnp.sum(named, axis=1, keepdims=True)
    busy = counts == jnp.max(counts, axis=0, keepdims=True)
    busiest = jnp.max(jnp.where(busy, names, 0)[:, :1], axis=0, keepdims=True)
    busiest_ref[...] = jnp.broadcast_to(busiest, busiest_ref.shape)
    cold = jnp.where(busy, 0.0, named)
    square = (rows, rows)
    first = lax.broadcasted_iota(jnp.int32, square, 0)
    second = lax.broadcasted_iota(jnp.int32, square, 1)
    before = jnp.where(first < second, 1.0, 0.0)
    rank = dot(cold.astype(bf16), before.astype(bf16), 1, 0)
    code = jnp.where(cold > 0.0, rank + 1.0, 0.0)
    hot_row = jnp.sum(jnp.where(busy, table, 0.0), axis=0, keepdims=True)
    hot_weight = jnp.sum(jnp.where(first == second, hot_row, 0.0), axis=1, keepdims=True)
    tokens = tokens_ref[...]
    cotangent = cotangent_ref[...]
    hot_ref[:, :features] = tokens
    hot_ref[:, features:] = (hot_weight * cotangent.astype(f32)).astype(bf16)

    owner = lax.broadcasted_iota(jnp.int32, (total, experts), 0) // 8
    spread = owner == lax.broadcasted_iota(jnp.int32, (total, experts), 1)
    spread = jnp.where(spread, 1.0, 0.0)
    code = dot(spread.astype(bf16), code.astype(bf16), 1, 0)
    table = dot(spread, table, 1, 0, highest)
    row = lax.broadcasted_iota(jnp.int32, (total, rows), 0)
    is_token = row % 8 < 4
    place = code == (row % 4 + 1).astype(f32)
    slot_weight = jnp.sum(jnp.where(place, table, 0.0), axis=1, keepdims=True)
    factor = jnp.where(is_token[:, :1], 1.0, slot_weight)
    place = jnp.where(place, 1.0, 0.0)
    picked = dot(jnp.where(is_token, place, 0.0).astype(bf16), tokens, 1, 0)
    picked = picked + dot(jnp.where(is_token, 0.0, place).astype(bf16), cotangent, 1, 0)
    out_ref[:, :features] = (picked * factor).astype(bf16)

    unit = shard_ref[0] * units + lax.broadcasted_iota(jnp.int32, (units, width), 0)
    choose = unit == lax.broadcasted_iota(jnp.int32, (units, width), 1)
    choose = jnp.where(choose, 1.0, 0.0).astype(bf16)
    pieces = [
        dot(choose, gate_ref[...], 1, 1),
        dot(choose, up_ref[...], 1, 1),
        dot(choose, down_ref[...], 1, 0),
    ]
    if height > 3 * units:
        pieces.append(jnp.zeros((height - 3 * units, features), f32))
    pieces = jnp.concatenate(pieces, axis=0).astype(bf16)
    for span in range(spans):
        out_ref[span * height : span * height + height, features:] = pieces[
            :, span * 256 : span * 256 + 256
        ]
    used = spans * height
    out_ref[used:, features:] = jnp.zeros((total - used, 256), bf16)


def pack(shard, tokens, cotangent, weight, routed, gate, up, down, experts, size):
    rows, features = tokens.shape
    return pl.pallas_call(
        functools.partial(pack_kernel, size=size),
        out_shape=(
            jax.ShapeDtypeStruct((experts * 8, features + 256), bf16),
            jax.ShapeDtypeStruct((rows, 2 * features), bf16),
            jax.ShapeDtypeStruct((8, 128), jnp.int32),
        ),
        in_specs=[pl.BlockSpec(memory_space=pltpu.SMEM)] + in_vmem(7),
        out_specs=tuple(in_vmem(3)),
        compiler_params=pltpu.CompilerParams(vmem_limit_bytes=48 * 2**20),
    )(shard, tokens, cotangent, weight, routed, gate, up, down)


def join_kernel(own_kept, own_came, hot_kept, hot_came, joined_ref, pair_ref):
    own_rows = own_kept.shape[1]
    rows = joined_ref.shape[1] - own_rows
    joined_ref[:, :own_rows, :] = add(own_kept[...], own_came[...])
    hot = add(hot_kept[...], hot_came[...])
    joined_ref[:, own_rows:, :] = hot[:, :rows]
    pair_ref[...] = hot[:, rows:]


def join(own_kept, own_came, hot_kept, hot_came, strip):
    depth, own_rows, _ = own_kept.shape
    rows = own_rows + hot_kept.shape[1] - strip
    return pl.pallas_call(
        join_kernel,
        out_shape=(
            jax.ShapeDtypeStruct((depth, rows, 128), bf16),
            jax.ShapeDtypeStruct((depth, strip, 128), bf16),
        ),
        in_specs=in_vmem(4),
        out_specs=tuple(in_vmem(2)),
        compiler_params=pltpu.CompilerParams(vmem_limit_bytes=48 * 2**20),
    )(own_kept, own_came, hot_kept, hot_came)


def pick_kernel(busiest_ref, piece_ref, out_ref):
    out_ref[...] = jnp.broadcast_to(piece_ref[...], out_ref.shape)


def pick(busiest, arrived, features):
    experts = arrived.shape[0]
    shape = (experts, 8, 256)
    grid_spec = pltpu.PrefetchScalarGridSpec(
        num_scalar_prefetch=1,
        grid=(1,),
        in_specs=[pl.BlockSpec((1, 8, 256), lambda i, chosen: (chosen[0], 0, features // 256))],
        out_specs=pl.BlockSpec(shape, lambda i, chosen: (0, 0, 0)),
    )
    return pl.pallas_call(
        pick_kernel, grid_spec=grid_spec, out_shape=jax.ShapeDtypeStruct(shape, bf16)
    )(busiest, arrived)


def total_kernel(parts_ref, out_ref):
    total = jnp.sum(parts_ref[...].astype(f32), axis=0, keepdims=True).astype(bf16)
    out_ref[...] = jnp.broadcast_to(total, out_ref.shape)


def total(back, half):
    shape = (back.shape[0], 8, 256)
    return pl.pallas_call(
        total_kernel,
        grid=(1,),
        in_specs=[pl.BlockSpec(shape, lambda i: (0, 0, half // 256))],
        out_specs=pl.BlockSpec(shape, lambda i: (0, 0, 0)),
        out_shape=jax.ShapeDtypeStruct(shape, bf16),
    )(back)


def own_kernel(
    core_ref, rows_ref, gate_ref, up_ref, down_ref, out_ref, kept_ref, passed_ref, grads, down_grads
):
    features, width = gate_ref.shape
    depth = kept_ref.shape[0]
    half = features // 2
    strip = features // (2 * depth)
    units = width // (2 * depth)
    lanes = width // 128
    core = core_ref[0]
    sides = ((kept_ref, core), (passed_ref, 1 - core))
    rows = rows_ref[:, :features]
    down = down_ref[...]
    gate_value = dot(rows, gate_ref[...], 1, 0)
    up_value = dot(rows, up_ref[...], 1, 0)
    upstream = dot(rows, down, 1, 1)
    count = gate_value.shape[0]
    upstream = pltpu.roll(upstream, count - 4, 0)
    sigmoid = jax.nn.sigmoid(gate_value)
    active = gate_value * sigmoid
    slope = sigmoid * (1.0 + gate_value * (1.0 - sigmoid))
    is_token = lax.broadcasted_iota(jnp.int32, (count, width), 0) % 8 < 4
    hidden = jnp.where(is_token, active * up_value, 0.0)
    shifted = pltpu.roll(hidden, 4, 0).astype(bf16)
    hidden = hidden.astype(bf16)
    gate_delta = jnp.where(is_token, upstream * up_value * slope, 0.0).astype(bf16)
    up_delta = jnp.where(is_token, upstream * active, 0.0).astype(bf16)
    for index, delta in enumerate((gate_delta, up_delta)):
        grads[...] = dot(rows, delta, 0, 0)
        for z in range(depth):
            for ref, side in sides:
                start = pl.multiple_of((2 * z + side) * strip, strip)
                block = grads[pl.ds(start, strip), :].astype(bf16)
                for lane in range(lanes):
                    at = (index * lanes + lane) * strip
                    ref[z, at : at + strip, :] = block[:, lane * 128 : lane * 128 + 128]
    down_grads[...] = dot(shifted, rows, 0, 0)
    base = 2 * lanes * strip
    for z in range(depth):
        for ref, side in sides:
            start = pl.multiple_of((2 * z + side) * units, 8)
            block = down_grads[pl.ds(start, units), :]
            for lane in range(0, features // 128, 2):
                at = base + lane * units
                pair = [block[:, i * 128 : i * 128 + 128] for i in (lane, lane + 1)]
                ref[z, at : at + 2 * units, :] = jnp.concatenate(pair, axis=0).astype(bf16)
    output = dot(hidden, down[:, :half], 1, 0) + dot(shifted, down[:, half:], 1, 0)
    out_ref[...] = output.astype(bf16)


def own_expert(core, rows, gate, up, down, depth):
    features, width = gate.shape
    side = jax.ShapeDtypeStruct((depth, 3 * features * width // (2 * depth) // 128, 128), bf16)
    return pl.pallas_call(
        own_kernel,
        out_shape=(jax.ShapeDtypeStruct((rows.shape[0], features // 2), bf16), side, side),
        in_specs=[pl.BlockSpec(memory_space=pltpu.SMEM)] + in_vmem(4),
        out_specs=tuple(in_vmem(3)),
        scratch_shapes=[pltpu.VMEM((features, width), f32), pltpu.VMEM((width, features), f32)],
        compiler_params=pltpu.CompilerParams(vmem_limit_bytes=48 * 2**20),
    )(core, rows, gate, up, down)


def hot_kernel(units, core_ref, rows_ref, blocks_ref, kept_ref, passed_ref, grads_ref, part, pair_part):
    features = part.shape[1]
    depth = kept_ref.shape[0]
    group = part.shape[0] // (2 * depth)
    spans = features // 256
    height = -(-3 * units // 16) * 16
    core = core_ref[0]
    inputs = rows_ref[:, :features]
    scaled = rows_ref[:, features:]
    sliced = jnp.concatenate(
        [blocks_ref[span * height : span * height + height, :] for span in range(spans)], axis=1
    )
    down = sliced[2 * units :]
    both = dot(sliced[: 2 * units], inputs, 1, 1)
    upstream = dot(down, scaled, 1, 1)[:units]
    gate_value, up_value = both[:units], both[units:]
    sigmoid = jax.nn.sigmoid(gate_value)
    active = gate_value * sigmoid
    slope = sigmoid * (1.0 + gate_value * (1.0 - sigmoid))
    pair = jnp.concatenate([upstream * up_value * slope, upstream * active], axis=0)
    spare = jnp.zeros((height - 3 * units, gate_value.shape[1]), f32)
    hidden = active * up_value
    if spare.shape[0]:
        hidden = jnp.concatenate([hidden, spare], axis=0)
    hidden = hidden.astype(bf16)
    part[...] = dot(hidden, down, 0, 0)
    empty = jnp.zeros_like(pair)
    spread = [jnp.where(core == 0, pair, empty), jnp.where(core == 1, pair, empty)]
    if 4 * units < 128:
        spread.append(jnp.zeros((128 - 4 * units, pair.shape[1]), f32))
    spread = jnp.concatenate(spread, axis=0).astype(bf16)
    pair_part[...] = dot(inputs, spread, 0, 1)
    strip = features // (2 * depth)
    wide = group * (features // 128)
    for z in range(depth):
        for ref, side in ((kept_ref, core), (passed_ref, 1 - core)):
            start = pl.multiple_of((2 * z + side) * group, group)
            block = part[pl.ds(start, group), :].astype(bf16)
            for lane in range(features // 128):
                ref[z, lane * group : lane * group + group, :] = block[
                    :, lane * 128 : lane * 128 + 128
                ]
            start = pl.multiple_of((2 * z + side) * strip, strip)
            ref[z, wide:, :] = pair_part[pl.ds(start, strip), :].astype(bf16)
    grads = dot(hidden, scaled, 1, 0)[:units]
    for lane in range(0, features // 128, 2):
        both = [grads[:, i * 128 : i * 128 + 128] for i in (lane, lane + 1)]
        grads_ref[lane * units : (lane + 2) * units, :] = jnp.concatenate(both, 0).astype(bf16)
    used = features // 128 * units
    grads_ref[used:, :] = jnp.zeros((grads_ref.shape[0] - used, 128), bf16)


def hot_expert(core, gathered, blocks, units, depth):
    total, features = gathered.shape[0], gathered.shape[1] // 2
    height = total // (2 * depth) * features // 128 + features // (2 * depth)
    side = jax.ShapeDtypeStruct((depth, height, 128), bf16)
    return pl.pallas_call(
        functools.partial(hot_kernel, units),
        out_shape=(side, side, jax.ShapeDtypeStruct((blocks.shape[0], 128), bf16)),
        in_specs=[pl.BlockSpec(memory_space=pltpu.SMEM)] + in_vmem(2),
        out_specs=tuple(in_vmem(3)),
        scratch_shapes=[pltpu.VMEM((total, features), f32), pltpu.VMEM((features, 128), f32)],
        compiler_params=pltpu.CompilerParams(vmem_limit_bytes=48 * 2**20),
    )(core, gathered, blocks)


def on_device(
    tokens, cotangent, route_weight, routed_experts, gate_weights, up_weights, down_weights
):
    experts = lax.axis_size("expert")
    size = lax.axis_size("dp")
    depth = size // 2
    mine = lax.axis_index("expert")
    shard = lax.axis_index("dp")
    core = shard % 2
    core_word = core.astype(jnp.int32).reshape(1)
    rows, features = tokens.shape
    half = features // 2
    gate, up, down = gate_weights[0], up_weights[0], down_weights[0]
    width = gate.shape[1]
    units = width // size
    strip = features // size

    shard_word = shard.astype(jnp.int32).reshape(1)
    outgoing, hot_rows, found = pack(
        shard_word,
        tokens,
        cotangent,
        route_weight.T,
        routed_experts.T,
        gate,
        up,
        down,
        experts,
        size,
    )
    gathered = lax.all_gather(hot_rows, "dp", axis=0, tiled=True)
    arrived = plane_exchange(outgoing.reshape(experts, 8, features + 256))
    picked = pick(found[0, :1], arrived, features)
    arrived, picked, routed, weight = lax.optimization_barrier(
        (arrived, picked, routed_experts.T, route_weight.T)
    )
    blocks = plane_exchange(picked)
    busiest, hits, table, place = routing(routed, weight, experts)
    is_token = (jnp.arange(8) < 4)[None, :, None]
    hot_weight = lax.dynamic_index_in_dim(table, busiest, 0, keepdims=False)
    wide_cotangent = cotangent.astype(f32)
    returning, own_kept, own_passed = own_expert(
        core_word, arrived.reshape(experts * 8, features + 256), gate, up, down, depth
    )
    blocks, own_passed = lax.optimization_barrier((blocks, own_passed))
    own_came = core_swap(own_passed)
    hot_kept, hot_passed, hot_grads = hot_expert(
        core_word, gathered, blocks.reshape(experts * 8, 256), units, depth
    )
    hot_came = core_swap(hot_passed)
    joined, pair = join(own_kept, own_came, hot_kept, hot_came, strip)
    summed = z_reduce_scatter(joined)[0]
    own_rows = own_kept.shape[1]
    own_sum = summed[:own_rows].astype(f32)
    hot_out = summed[own_rows:].reshape(features // 128, rows, 128)
    hot_out = hot_out.transpose(1, 0, 2).reshape(rows, features)
    pair = pad_blocks(z_exchange(pair).reshape(depth * strip // 8, 8, 128), experts)

    back = plane_exchange(
        jnp.concatenate(
            [returning.reshape(experts, 8, half), pair, hot_grads.reshape(experts, 8, 128)], axis=2
        )
    )
    hot_blocks = plane_exchange(total(back, half))

    lane = np.arange(depth * 128)
    within = lane % 128
    column = (within % (2 * units)) // units * width
    column = column + (lane // 128 * 2 + within // (2 * units)) * units + within % units
    column = np.where(within < 4 * units, column, -1).astype(np.int32)
    spread = (jnp.asarray(column)[:, None] == jnp.arange(2 * width, dtype=jnp.int32)).astype(bf16)
    hot_pair = hot_blocks[: depth * strip // 8, :, :128].reshape(depth, strip, 128)
    hot_pair = dot(hot_pair.transpose(1, 0, 2).reshape(strip, depth * 128), spread, 1, 0)
    hot_down = hot_blocks.reshape(experts * 8, 256)[: features // 128 * units, 128:]
    hot_down = hot_down.reshape(features // 128, units, 128).transpose(1, 0, 2)
    hot_down = hot_down.reshape(units, features).astype(f32)

    results = back[:, :, :half].reshape(experts * 8, half)
    weighting = jnp.where(place, table[:, None, :], 0.0)
    halves = jnp.concatenate(
        [jnp.where(is_token, weighting, 0.0), jnp.where(is_token, 0.0, weighting)], axis=2
    ).reshape(experts * 8, 2 * rows)
    weighed = dot(halves, results.astype(f32), 0, 0, highest)
    wide_hot = hot_out.astype(f32)
    layer_out = jnp.concatenate([weighed[:rows], weighed[rows:]], axis=1)
    layer_out = (layer_out + hot_weight[:, None] * wide_hot).astype(bf16)

    products = jnp.where(
        is_token,
        dot(results, cotangent[:, :half], 1, 1).reshape(experts, 8, rows),
        dot(results, cotangent[:, half:], 1, 1).reshape(experts, 8, rows),
    )
    by_expert = jnp.sum(jnp.where(place, products, 0.0), axis=1)
    hot_product = jnp.sum(wide_hot * wide_cotangent, axis=1)
    is_busiest = jnp.arange(experts, dtype=jnp.int32)[:, None] == busiest
    by_expert = by_expert + jnp.where(is_busiest, hot_product[None], 0.0)
    route_gradient = jnp.sum(jnp.where(hits, by_expert[:, None, :], 0.0), axis=0).T

    def unstripe(block, tall):
        return block.reshape(-1, tall, 128).transpose(1, 0, 2).reshape(tall, -1)

    count = strip * width // 128
    home = mine == busiest
    gate_gradient = unstripe(own_sum[:count], strip) + jnp.where(
        home, hot_pair[:, :width], 0.0
    )
    up_gradient = unstripe(own_sum[count : 2 * count], strip) + jnp.where(
        home, hot_pair[:, width:], 0.0
    )
    down_gradient = unstripe(own_sum[2 * count :], units) + jnp.where(home, hot_down, 0.0)
    return (layer_out, route_gradient, gate_gradient[None], up_gradient[None], down_gradient[None])


def solution(mesh):
    in_specs = (
        P(("dp", "expert"), None),
        P(("dp", "expert"), None),
        P(("dp", "expert"), None),
        P(("dp", "expert"), None),
        P("expert", None, None),
        P("expert", None, None),
        P("expert", None, None),
    )
    out_specs = (
        P(("dp", "expert"), None),
        P(("dp", "expert"), None),
        P("expert", "dp", None),
        P("expert", "dp", None),
        P("expert", "dp", None),
    )
    return jax.shard_map(
        on_device, mesh=mesh, in_specs=in_specs, out_specs=out_specs, check_vma=False
    )
```

```python
import functools

import jax
import jax.numpy as jnp
from jax import lax
from jax.experimental import pallas as pl
from jax.experimental.pallas import tpu as pltpu
from jax.sharding import PartitionSpec as P

f32 = jnp.float32
bf16 = jnp.bfloat16
highest = lax.Precision.HIGHEST


def dot(lhs, rhs, lhs_dim, rhs_dim, precision=None):
    dims = (((lhs_dim,), (rhs_dim,)), ((), ()))
    return lax.dot_general(lhs, rhs, dims, precision=precision, preferred_element_type=f32)


def plane_exchange(blocks):
    return lax.all_to_all(blocks, "expert", split_axis=0, concat_axis=0, tiled=True)


def core_swap(block):
    size = lax.axis_size("dp")
    return lax.ppermute(block, "dp", [(i, i ^ 1) for i in range(size)])


def z_exchange(blocks):
    size = lax.axis_size("dp")
    groups = [list(range(core, size, 2)) for core in range(2)]
    return lax.all_to_all(
        blocks, "dp", split_axis=0, concat_axis=0, tiled=True, axis_index_groups=groups
    )


def z_reduce_scatter(blocks):
    size = lax.axis_size("dp")
    groups = [list(range(core, size, 2)) for core in range(2)]
    return lax.psum_scatter(
        blocks, "dp", scatter_dimension=0, tiled=True, axis_index_groups=groups
    )


def add(one, other):
    return (one.astype(f32) + other.astype(f32)).astype(bf16)


def pad_blocks(blocks, count):
    return jnp.pad(blocks, ((0, count - blocks.shape[0]),) + ((0, 0),) * (blocks.ndim - 1))


def in_vmem(count):
    return [pl.BlockSpec(memory_space=pltpu.VMEM)] * count


def tables(routed_ref, weight_ref, experts):
    rows = routed_ref.shape[1]
    total = experts * 8
    names = lax.broadcasted_iota(jnp.int32, (experts, rows), 0)
    named = jnp.zeros((experts, rows), f32)
    table = jnp.zeros((experts, rows), f32)
    for k in range(routed_ref.shape[0]):
        hit = routed_ref[k : k + 1, :] == names
        named = jnp.where(hit, 1.0, named)
        table = jnp.where(hit, weight_ref[k : k + 1, :], table)
    counts = jnp.sum(named, axis=1, keepdims=True)
    busy = counts == jnp.max(counts, axis=0, keepdims=True)
    busiest = jnp.max(jnp.where(busy, names, 0)[:, :1], axis=0, keepdims=True)
    cold = jnp.where(busy, 0.0, named)
    first = lax.broadcasted_iota(jnp.int32, (rows, rows), 0)
    second = lax.broadcasted_iota(jnp.int32, (rows, rows), 1)
    before = jnp.where(first < second, 1.0, 0.0)
    rank = dot(cold.astype(bf16), before.astype(bf16), 1, 0)
    code = jnp.where(cold > 0.0, rank + 1.0, 0.0)
    hot_row = jnp.sum(jnp.where(busy, table, 0.0), axis=0, keepdims=True)
    hot_weight = jnp.sum(jnp.where(first == second, hot_row, 0.0), axis=1, keepdims=True)
    owner = lax.broadcasted_iota(jnp.int32, (total, experts), 0) // 8
    spread = owner == lax.broadcasted_iota(jnp.int32, (total, experts), 1)
    spread = jnp.where(spread, 1.0, 0.0)
    code = dot(spread.astype(bf16), code.astype(bf16), 1, 0)
    table = dot(spread, table, 1, 0, highest)
    row = lax.broadcasted_iota(jnp.int32, (total, rows), 0)
    is_token = row % 8 < 4
    place = code == (row % 4 + 1).astype(f32)
    return hot_weight, busiest, place, is_token, jnp.where(place, table, 0.0)


def pack_kernel(
    shard_ref, routed_hbm, weight_hbm, tokens_hbm, cotangent_hbm, gate_hbm, up_hbm, down_hbm, out_ref, hot_ref, busiest_ref,
    tokens_ref, cotangent_ref, weight_ref, routed_ref, gate_ref, up_ref, down_ref, sems, size
):
    moves = []
    sources = (routed_hbm, weight_hbm, tokens_hbm, cotangent_hbm, gate_hbm, up_hbm, down_hbm)
    targets = (routed_ref, weight_ref, tokens_ref, cotangent_ref, gate_ref, up_ref, down_ref)
    for index, (source, target) in enumerate(zip(sources, targets)):
        moves.append(pltpu.make_async_copy(source, target, sems.at[index]))
        moves[index].start()
    rows, features = tokens_ref.shape
    width = gate_ref.shape[1]
    units = width // size
    height, spans = -(-3 * units // 16) * 16, features // 256
    total = out_ref.shape[0]
    experts = total // 8
    moves[0].wait()
    moves[1].wait()
    hot_weight, busiest, place, is_token, spots = tables(routed_ref, weight_ref, experts)
    busiest_ref[...] = jnp.broadcast_to(busiest, busiest_ref.shape)
    moves[2].wait()
    moves[3].wait()
    tokens = tokens_ref[...]
    cotangent = cotangent_ref[...]
    hot_ref[:, :features] = tokens
    hot_ref[:, features:] = (hot_weight * cotangent.astype(f32)).astype(bf16)

    slot_weight = jnp.sum(spots, axis=1, keepdims=True)
    factor = jnp.where(is_token[:, :1], 1.0, slot_weight)
    place = jnp.where(place, 1.0, 0.0)
    picked = dot(jnp.where(is_token, place, 0.0).astype(bf16), tokens, 1, 0)
    picked = picked + dot(jnp.where(is_token, 0.0, place).astype(bf16), cotangent, 1, 0)
    out_ref[:, :features] = (picked * factor).astype(bf16)

    unit = shard_ref[0] * units + lax.broadcasted_iota(jnp.int32, (units, width), 0)
    choose = unit == lax.broadcasted_iota(jnp.int32, (units, width), 1)
    choose = jnp.where(choose, 1.0, 0.0).astype(bf16)
    for move in moves[4:]:
        move.wait()
    pieces = [
        dot(choose, gate_ref[...], 1, 1),
        dot(choose, up_ref[...], 1, 1),
        dot(choose, down_ref[...], 1, 0),
    ]
    if height > 3 * units:
        pieces.append(jnp.zeros((height - 3 * units, features), f32))
    pieces = jnp.concatenate(pieces, axis=0).astype(bf16)
    for span in range(spans):
        out_ref[span * height : span * height + height, features:] = pieces[
            :, span * 256 : span * 256 + 256
        ]
    used = spans * height
    out_ref[used:, features:] = jnp.zeros((total - used, 256), bf16)


def pack(shard, tokens, cotangent, weight, routed, gate, up, down, experts, size):
    rows, features = tokens.shape
    return pl.pallas_call(
        functools.partial(pack_kernel, size=size),
        out_shape=(
            jax.ShapeDtypeStruct((experts * 8, features + 256), bf16),
            jax.ShapeDtypeStruct((rows, 2 * features), bf16),
            jax.ShapeDtypeStruct((8, 128), jnp.int32),
        ),
        in_specs=[pl.BlockSpec(memory_space=pltpu.SMEM)]
        + [pl.BlockSpec(memory_space=pl.ANY)] * 7,
        out_specs=tuple(in_vmem(3)),
        scratch_shapes=[
            pltpu.VMEM((rows, features), bf16),
            pltpu.VMEM((rows, features), bf16),
            pltpu.VMEM(weight.shape, f32),
            pltpu.VMEM(routed.shape, jnp.int32),
            pltpu.VMEM(gate.shape, bf16),
            pltpu.VMEM(up.shape, bf16),
            pltpu.VMEM(down.shape, bf16),
            pltpu.SemaphoreType.DMA((7,)),
        ],
        compiler_params=pltpu.CompilerParams(vmem_limit_bytes=48 * 2**20),
    )(shard, routed, weight, tokens, cotangent, gate, up, down)


def join_kernel(own_kept, own_came, hot_kept, hot_came, joined_ref, pair_ref):
    own_rows = own_kept.shape[1]
    rows = joined_ref.shape[1] - own_rows
    joined_ref[:, :own_rows, :] = add(own_kept[...], own_came[...])
    hot = add(hot_kept[...], hot_came[...])
    joined_ref[:, own_rows:, :] = hot[:, :rows]
    pair_ref[...] = hot[:, rows:]


def join(own_kept, own_came, hot_kept, hot_came, strip):
    depth, own_rows, _ = own_kept.shape
    rows = own_rows + hot_kept.shape[1] - strip
    return pl.pallas_call(
        join_kernel,
        out_shape=(
            jax.ShapeDtypeStruct((depth, rows, 128), bf16),
            jax.ShapeDtypeStruct((depth, strip, 128), bf16),
        ),
        in_specs=in_vmem(4),
        out_specs=tuple(in_vmem(2)),
        compiler_params=pltpu.CompilerParams(vmem_limit_bytes=48 * 2**20),
    )(own_kept, own_came, hot_kept, hot_came)


def pick_kernel(busiest_ref, piece_ref, out_ref):
    out_ref[...] = jnp.broadcast_to(piece_ref[...], out_ref.shape)


def pick(busiest, arrived, features):
    experts = arrived.shape[0]
    shape = (experts, 8, 256)
    grid_spec = pltpu.PrefetchScalarGridSpec(
        num_scalar_prefetch=1,
        grid=(1,),
        in_specs=[pl.BlockSpec((1, 8, 256), lambda i, chosen: (chosen[0], 0, features // 256))],
        out_specs=pl.BlockSpec(shape, lambda i, chosen: (0, 0, 0)),
    )
    return pl.pallas_call(
        pick_kernel, grid_spec=grid_spec, out_shape=jax.ShapeDtypeStruct(shape, bf16)
    )(busiest, arrived)


def total_kernel(parts_ref, out_ref):
    half = parts_ref.shape[2] - 256
    sums = jnp.sum(parts_ref[:, :, half:].astype(f32), axis=0, keepdims=True).astype(bf16)
    out_ref[...] = jnp.broadcast_to(sums, out_ref.shape)


def total(back):
    return pl.pallas_call(
        total_kernel,
        in_specs=in_vmem(1),
        out_specs=in_vmem(1)[0],
        out_shape=jax.ShapeDtypeStruct((back.shape[0], 8, 256), bf16),
    )(back)


def own_kernel(
    core_ref, rows_ref, gate_ref, up_ref, down_ref, out_ref, kept_ref, passed_ref, grads, down_grads
):
    features, width = gate_ref.shape
    depth = kept_ref.shape[0]
    half = features // 2
    strip = features // (2 * depth)
    units = width // (2 * depth)
    lanes = width // 128
    core = core_ref[0]
    sides = ((kept_ref, core), (passed_ref, 1 - core))
    rows = rows_ref[:, :features]
    down = down_ref[...]
    gate_value = dot(rows, gate_ref[...], 1, 0)
    up_value = dot(rows, up_ref[...], 1, 0)
    upstream = dot(rows, down, 1, 1)
    count = gate_value.shape[0]
    upstream = pltpu.roll(upstream, count - 4, 0)
    sigmoid = jax.nn.sigmoid(gate_value)
    active = gate_value * sigmoid
    slope = sigmoid * (1.0 + gate_value * (1.0 - sigmoid))
    is_token = lax.broadcasted_iota(jnp.int32, (count, width), 0) % 8 < 4
    hidden = jnp.where(is_token, active * up_value, 0.0)
    shifted = pltpu.roll(hidden, 4, 0).astype(bf16)
    hidden = hidden.astype(bf16)
    gate_delta = jnp.where(is_token, upstream * up_value * slope, 0.0).astype(bf16)
    up_delta = jnp.where(is_token, upstream * active, 0.0).astype(bf16)
    for index, delta in enumerate((gate_delta, up_delta)):
        grads[...] = dot(rows, delta, 0, 0)
        for z in range(depth):
            for ref, side in sides:
                start = pl.multiple_of((2 * z + side) * strip, strip)
                block = grads[pl.ds(start, strip), :].astype(bf16)
                for lane in range(lanes):
                    at = (index * lanes + lane) * strip
                    ref[z, at : at + strip, :] = block[:, lane * 128 : lane * 128 + 128]
    down_grads[...] = dot(shifted, rows, 0, 0)
    base = 2 * lanes * strip
    for z in range(depth):
        for ref, side in sides:
            start = pl.multiple_of((2 * z + side) * units, 8)
            block = down_grads[pl.ds(start, units), :]
            for lane in range(0, features // 128, 2):
                at = base + lane * units
                pair = [block[:, i * 128 : i * 128 + 128] for i in (lane, lane + 1)]
                ref[z, at : at + 2 * units, :] = jnp.concatenate(pair, axis=0).astype(bf16)
    output = dot(hidden, down[:, :half], 1, 0) + dot(shifted, down[:, half:], 1, 0)
    out_ref[...] = output.astype(bf16)


def own_expert(core, rows, gate, up, down, depth):
    features, width = gate.shape
    side = jax.ShapeDtypeStruct((depth, 3 * features * width // (2 * depth) // 128, 128), bf16)
    return pl.pallas_call(
        own_kernel,
        out_shape=(jax.ShapeDtypeStruct((rows.shape[0], features // 2), bf16), side, side),
        in_specs=[pl.BlockSpec(memory_space=pltpu.SMEM)] + in_vmem(4),
        out_specs=tuple(in_vmem(3)),
        scratch_shapes=[pltpu.VMEM((features, width), f32), pltpu.VMEM((width, features), f32)],
        compiler_params=pltpu.CompilerParams(vmem_limit_bytes=48 * 2**20),
    )(core, rows, gate, up, down)


def hot_kernel(
    units, core_ref, rows_hbm, blocks_ref, kept_ref, passed_ref, grads_ref, part, pair_part, inputs_ref, scaled_ref, sems
):
    features = part.shape[1]
    depth = kept_ref.shape[0]
    group = part.shape[0] // (2 * depth)
    spans = features // 256
    height = -(-3 * units // 16) * 16
    core = core_ref[0]
    first = pltpu.make_async_copy(rows_hbm.at[:, :features], inputs_ref, sems.at[0])
    second = pltpu.make_async_copy(rows_hbm.at[:, features:], scaled_ref, sems.at[1])
    first.start()
    second.start()
    sliced = jnp.concatenate(
        [blocks_ref[span * height : span * height + height, :] for span in range(spans)], axis=1
    )
    down = sliced[2 * units :]
    first.wait()
    inputs = inputs_ref[...]
    both = dot(sliced[: 2 * units], inputs, 1, 1)
    second.wait()
    scaled = scaled_ref[...]
    upstream = dot(down, scaled, 1, 1)[:units]
    gate_value, up_value = both[:units], both[units:]
    sigmoid = jax.nn.sigmoid(gate_value)
    active = gate_value * sigmoid
    slope = sigmoid * (1.0 + gate_value * (1.0 - sigmoid))
    pair = jnp.concatenate([upstream * up_value * slope, upstream * active], axis=0)
    spare = jnp.zeros((height - 3 * units, gate_value.shape[1]), f32)
    hidden = active * up_value
    if spare.shape[0]:
        hidden = jnp.concatenate([hidden, spare], axis=0)
    hidden = hidden.astype(bf16)
    part[...] = dot(hidden, down, 0, 0)
    empty = jnp.zeros_like(pair)
    spread = [jnp.where(core == 0, pair, empty), jnp.where(core == 1, pair, empty)]
    if 4 * units < 128:
        spread.append(jnp.zeros((128 - 4 * units, pair.shape[1]), f32))
    spread = jnp.concatenate(spread, axis=0).astype(bf16)
    pair_part[...] = dot(inputs, spread, 0, 1)
    strip = features // (2 * depth)
    wide = group * (features // 128)
    for z in range(depth):
        for ref, side in ((kept_ref, core), (passed_ref, 1 - core)):
            start = pl.multiple_of((2 * z + side) * group, group)
            block = part[pl.ds(start, group), :].astype(bf16)
            for lane in range(features // 128):
                ref[z, lane * group : lane * group + group, :] = block[
                    :, lane * 128 : lane * 128 + 128
                ]
            start = pl.multiple_of((2 * z + side) * strip, strip)
            ref[z, wide:, :] = pair_part[pl.ds(start, strip), :].astype(bf16)
    grads = dot(hidden, scaled, 1, 0)[:units]
    for lane in range(0, features // 128, 2):
        both = [grads[:, i * 128 : i * 128 + 128] for i in (lane, lane + 1)]
        grads_ref[lane * units : (lane + 2) * units, :] = jnp.concatenate(both, 0).astype(bf16)
    used = features // 128 * units
    grads_ref[used:, :] = jnp.zeros((grads_ref.shape[0] - used, 128), bf16)


def hot_expert(core, gathered, blocks, units, depth):
    total, features = gathered.shape[0], gathered.shape[1] // 2
    height = total // (2 * depth) * features // 128 + features // (2 * depth)
    side = jax.ShapeDtypeStruct((depth, height, 128), bf16)
    return pl.pallas_call(
        functools.partial(hot_kernel, units),
        out_shape=(side, side, jax.ShapeDtypeStruct((blocks.shape[0], 128), bf16)),
        in_specs=[pl.BlockSpec(memory_space=pltpu.SMEM), pl.BlockSpec(memory_space=pl.ANY)]
        + in_vmem(1),
        out_specs=tuple(in_vmem(3)),
        scratch_shapes=[
            pltpu.VMEM((total, features), f32),
            pltpu.VMEM((features, 128), f32),
            pltpu.VMEM((total, features), bf16),
            pltpu.VMEM((total, features), bf16),
            pltpu.SemaphoreType.DMA((2,)),
        ],
        compiler_params=pltpu.CompilerParams(vmem_limit_bytes=48 * 2**20),
    )(core, gathered, blocks)


def middle_kernel(
    units, routed_ref, weight_ref, cotangent_ref, back_ref, summed_ref,
    layer_ref, route_ref, gate_ref, up_ref, down_ref, spread_ref
):
    rows, features = cotangent_ref.shape
    half = features // 2
    strip, width = gate_ref.shape
    experts = back_ref.shape[0] // 8
    hot_weight, busiest, place, is_token, spots = tables(routed_ref, weight_ref, experts)
    cotangent = cotangent_ref[...]
    results = back_ref[:, :half]
    own_rows = summed_ref.shape[0] - rows * (features // 128)
    blocks = [
        summed_ref[own_rows + i * rows : own_rows + (i + 1) * rows, :]
        for i in range(features // 128)
    ]
    hot_out = jnp.concatenate(blocks, axis=1).astype(f32)
    sides = []
    for side in (jnp.where(is_token, spots, 0.0), jnp.where(is_token, 0.0, spots)):
        high = side.astype(bf16)
        low = (side - high.astype(f32)).astype(bf16)
        sides.append(dot(high, results, 0, 0) + dot(low, results, 0, 0))
    layer = jnp.concatenate(sides, axis=1) + hot_weight * hot_out
    layer_ref[...] = layer.astype(bf16)

    left = dot(results, cotangent[:, :half], 1, 1)
    right = dot(results, cotangent[:, half:], 1, 1)
    products = jnp.where(place, jnp.where(is_token, left, right), 0.0)
    hot_column = jnp.sum(hot_out * cotangent.astype(f32), axis=1, keepdims=True)
    first = lax.broadcasted_iota(jnp.int32, (rows, rows), 0)
    second = lax.broadcasted_iota(jnp.int32, (rows, rows), 1)
    hot_row = jnp.sum(jnp.where(first == second, hot_column, 0.0), axis=0, keepdims=True)
    owner = lax.broadcasted_iota(jnp.int32, products.shape, 0) // 8
    for k in range(routed_ref.shape[0]):
        named = routed_ref[k : k + 1, :]
        cold = jnp.sum(jnp.where(owner == named, products, 0.0), axis=0, keepdims=True)
        route_ref[k : k + 1, :] = cold + jnp.where(named == busiest, hot_row, 0.0)

    lanes = width // 128
    for index, ref in enumerate((gate_ref, up_ref)):
        for lane in range(lanes):
            at = (index * lanes + lane) * strip
            ref[:, lane * 128 : lane * 128 + 128] = summed_ref[at : at + strip, :].astype(f32)
    base = 2 * lanes * strip
    unpair(down_ref, summed_ref, base, 0, units)

    shape = (spread_ref.shape[0], 2 * width)
    lane = lax.broadcasted_iota(jnp.int32, (shape[0], 1), 0)
    within = lane % 128
    column = (within % (2 * units)) // units * width + within % units
    column = column + (lane // 128 * 2 + within // (2 * units)) * units
    column = jnp.where(within < 4 * units, column, -1)
    match = lax.broadcasted_iota(jnp.int32, shape, 1) == column
    spread_ref[...] = jnp.where(match, 1.0, 0.0).astype(bf16)


def unpair(out_ref, from_ref, base, lane_base, units):
    for lane in range(0, out_ref.shape[1] // 128, 2):
        at = base + lane * units
        pair = from_ref[at : at + 2 * units, lane_base : lane_base + 128].astype(f32)
        out_ref[:, lane * 128 : lane * 128 + 128] = pair[:units]
        out_ref[:, lane * 128 + 128 : lane * 128 + 256] = pair[units:]


def middle(routed, weight, cotangent, back, summed, units, strip, depth):
    rows, features = cotangent.shape
    width = units * 2 * depth
    return pl.pallas_call(
        functools.partial(middle_kernel, units),
        out_shape=(
            jax.ShapeDtypeStruct((rows, features), bf16),
            jax.ShapeDtypeStruct(weight.shape, f32),
            jax.ShapeDtypeStruct((strip, width), f32),
            jax.ShapeDtypeStruct((strip, width), f32),
            jax.ShapeDtypeStruct((units, features), f32),
            jax.ShapeDtypeStruct((depth * 128, 2 * width), bf16),
        ),
        in_specs=in_vmem(5),
        out_specs=tuple(in_vmem(6)),
        compiler_params=pltpu.CompilerParams(vmem_limit_bytes=48 * 2**20),
    )(routed, weight, cotangent, back, summed)


def last_kernel(
    units, home_ref, blocks_ref, gate_ref, up_ref, down_ref, spread_ref,
    gate_out, up_out, down_out, scratch
):
    strip, width = gate_ref.shape
    depth = spread_ref.shape[0] // 128
    home = home_ref[0] == 1
    blocks = [blocks_ref[z * strip : (z + 1) * strip, :128] for z in range(depth)]
    pair = dot(jnp.concatenate(blocks, axis=1), spread_ref[...], 1, 0)
    gate_out[...] = gate_ref[...] + jnp.where(home, pair[:, :width], 0.0)
    up_out[...] = up_ref[...] + jnp.where(home, pair[:, width:], 0.0)
    unpair(scratch, blocks_ref, 0, 128, units)
    down_out[...] = down_ref[...] + jnp.where(home, scratch[...], 0.0)


def last(home, blocks, gate, up, down, spread):
    units = down.shape[0]
    return pl.pallas_call(
        functools.partial(last_kernel, units),
        out_shape=tuple(jax.ShapeDtypeStruct(x.shape, f32) for x in (gate, up, down)),
        in_specs=[pl.BlockSpec(memory_space=pltpu.SMEM)] + in_vmem(5),
        out_specs=tuple(in_vmem(3)),
        scratch_shapes=[pltpu.VMEM(down.shape, f32)],
        compiler_params=pltpu.CompilerParams(vmem_limit_bytes=48 * 2**20),
    )(home, blocks, gate, up, down, spread)


def on_device(
    tokens, cotangent, route_weight, routed_experts, gate_weights, up_weights, down_weights
):
    experts = lax.axis_size("expert")
    size = lax.axis_size("dp")
    depth = size // 2
    mine = lax.axis_index("expert")
    shard = lax.axis_index("dp")
    core = shard % 2
    core_word = core.astype(jnp.int32).reshape(1)
    rows, features = tokens.shape
    half = features // 2
    gate, up, down = gate_weights[0], up_weights[0], down_weights[0]
    width = gate.shape[1]
    units = width // size
    strip = features // size

    shard_word = shard.astype(jnp.int32).reshape(1)
    outgoing, hot_rows, found = pack(
        shard_word,
        tokens,
        cotangent,
        route_weight.T,
        routed_experts.T,
        gate,
        up,
        down,
        experts,
        size,
    )
    gathered = lax.all_gather(hot_rows, "dp", axis=0, tiled=True)
    arrived = plane_exchange(outgoing.reshape(experts, 8, features + 256))
    picked = pick(found[0, :1], arrived, features)
    arrived, picked, routed, weight = lax.optimization_barrier(
        (arrived, picked, routed_experts.T, route_weight.T)
    )
    blocks = plane_exchange(picked)
    returning, own_kept, own_passed = own_expert(
        core_word, arrived.reshape(experts * 8, features + 256), gate, up, down, depth
    )
    blocks, own_passed = lax.optimization_barrier((blocks, own_passed))
    own_came = core_swap(own_passed)
    hot_kept, hot_passed, hot_grads = hot_expert(
        core_word, gathered, blocks.reshape(experts * 8, 256), units, depth
    )
    hot_came = core_swap(hot_passed)
    joined, pair = join(own_kept, own_came, hot_kept, hot_came, strip)
    summed = z_reduce_scatter(joined)[0]
    pair = pad_blocks(z_exchange(pair).reshape(depth * strip // 8, 8, 128), experts)

    back = plane_exchange(
        jnp.concatenate(
            [returning.reshape(experts, 8, half), pair, hot_grads.reshape(experts, 8, 128)], axis=2
        )
    )
    hot_blocks = plane_exchange(total(back))
    layer_out, route_gradient, own_gate, own_up, own_down, spread = middle(
        routed, weight, cotangent, back.reshape(experts * 8, -1), summed, units, strip, depth
    )
    home = (mine == found[0, 0]).astype(jnp.int32).reshape(1)
    gate_gradient, up_gradient, down_gradient = last(
        home, hot_blocks.reshape(experts * 8, 256), own_gate, own_up, own_down, spread
    )
    return (
        layer_out,
        route_gradient.T,
        gate_gradient[None],
        up_gradient[None],
        down_gradient[None],
    )


def solution(mesh):
    in_specs = (
        P(("dp", "expert"), None),
        P(("dp", "expert"), None),
        P(("dp", "expert"), None),
        P(("dp", "expert"), None),
        P("expert", None, None),
        P("expert", None, None),
        P("expert", None, None),
    )
    out_specs = (
        P(("dp", "expert"), None),
        P(("dp", "expert"), None),
        P("expert", "dp", None),
        P("expert", "dp", None),
        P("expert", "dp", None),
    )
    return jax.shard_map(
        on_device, mesh=mesh, in_specs=in_specs, out_specs=out_specs, check_vma=False
    )
```

```python
import functools

import jax
import jax.numpy as jnp
from jax import lax
from jax.experimental import pallas as pl
from jax.experimental.pallas import tpu as pltpu
from jax.sharding import PartitionSpec as P

f32 = jnp.float32
bf16 = jnp.bfloat16
highest = lax.Precision.HIGHEST


def dot(lhs, rhs, lhs_dim, rhs_dim, precision=None):
    dims = (((lhs_dim,), (rhs_dim,)), ((), ()))
    return lax.dot_general(lhs, rhs, dims, precision=precision, preferred_element_type=f32)


def plane_exchange(blocks):
    return lax.all_to_all(blocks, "expert", split_axis=0, concat_axis=0, tiled=True)


def core_swap(block):
    size = lax.axis_size("dp")
    return lax.ppermute(block, "dp", [(i, i ^ 1) for i in range(size)])


def z_exchange(blocks):
    size = lax.axis_size("dp")
    groups = [list(range(core, size, 2)) for core in range(2)]
    return lax.all_to_all(
        blocks, "dp", split_axis=0, concat_axis=0, tiled=True, axis_index_groups=groups
    )


def z_reduce_scatter(blocks):
    size = lax.axis_size("dp")
    groups = [list(range(core, size, 2)) for core in range(2)]
    return lax.psum_scatter(
        blocks, "dp", scatter_dimension=0, tiled=True, axis_index_groups=groups
    )


def add(one, other):
    return (one.astype(f32) + other.astype(f32)).astype(bf16)


def pad_blocks(blocks, count):
    return jnp.pad(blocks, ((0, count - blocks.shape[0]),) + ((0, 0),) * (blocks.ndim - 1))


def in_vmem(count):
    return [pl.BlockSpec(memory_space=pltpu.VMEM)] * count


def tables(routed_ref, weight_ref, experts):
    rows = routed_ref.shape[1]
    total = experts * 8
    names = lax.broadcasted_iota(jnp.int32, (experts, rows), 0)
    named = jnp.zeros((experts, rows), f32)
    table = jnp.zeros((experts, rows), f32)
    for k in range(routed_ref.shape[0]):
        hit = routed_ref[k : k + 1, :] == names
        named = jnp.where(hit, 1.0, named)
        table = jnp.where(hit, weight_ref[k : k + 1, :], table)
    counts = jnp.sum(named, axis=1, keepdims=True)
    busy = counts == jnp.max(counts, axis=0, keepdims=True)
    busiest = jnp.max(jnp.where(busy, names, 0)[:, :1], axis=0, keepdims=True)
    cold = jnp.where(busy, 0.0, named)
    first = lax.broadcasted_iota(jnp.int32, (rows, rows), 0)
    second = lax.broadcasted_iota(jnp.int32, (rows, rows), 1)
    before = jnp.where(first < second, 1.0, 0.0)
    rank = dot(cold.astype(bf16), before.astype(bf16), 1, 0)
    code = jnp.where(cold > 0.0, rank + 1.0, 0.0)
    hot_row = jnp.sum(jnp.where(busy, table, 0.0), axis=0, keepdims=True)
    hot_weight = jnp.sum(jnp.where(first == second, hot_row, 0.0), axis=1, keepdims=True)
    owner = lax.broadcasted_iota(jnp.int32, (total, experts), 0) // 8
    spread = owner == lax.broadcasted_iota(jnp.int32, (total, experts), 1)
    spread = jnp.where(spread, 1.0, 0.0)
    code = dot(spread.astype(bf16), code.astype(bf16), 1, 0)
    table = dot(spread, table, 1, 0, highest)
    row = lax.broadcasted_iota(jnp.int32, (total, rows), 0)
    is_token = row % 8 < 4
    place = code == (row % 4 + 1).astype(f32)
    return hot_weight, busiest, place, is_token, jnp.where(place, table, 0.0)


def pack_kernel(
    shard_ref, routed_hbm, weight_hbm, tokens_hbm, cotangent_hbm, gate_hbm, up_hbm, down_hbm, out_ref, hot_ref, busiest_ref,
    tokens_ref, cotangent_ref, weight_ref, routed_ref, gate_ref, up_ref, down_ref, sems, size
):
    moves = []
    sources = (routed_hbm, weight_hbm, tokens_hbm, cotangent_hbm, gate_hbm, up_hbm, down_hbm)
    targets = (routed_ref, weight_ref, tokens_ref, cotangent_ref, gate_ref, up_ref, down_ref)
    for index, (source, target) in enumerate(zip(sources, targets)):
        moves.append(pltpu.make_async_copy(source, target, sems.at[index]))
        moves[index].start()
    rows, features = tokens_ref.shape
    width = gate_ref.shape[1]
    units = width // size
    height, spans = -(-3 * units // 16) * 16, features // 256
    total = out_ref.shape[0]
    experts = total // 8
    moves[0].wait()
    moves[1].wait()
    hot_weight, busiest, place, is_token, spots = tables(routed_ref, weight_ref, experts)
    busiest_ref[...] = jnp.broadcast_to(busiest, busiest_ref.shape)
    moves[2].wait()
    moves[3].wait()
    tokens = tokens_ref[...]
    cotangent = cotangent_ref[...]
    hot_ref[:, :features] = tokens
    hot_ref[:, features:] = (hot_weight * cotangent.astype(f32)).astype(bf16)

    slot_weight = jnp.sum(spots, axis=1, keepdims=True)
    factor = jnp.where(is_token[:, :1], 1.0, slot_weight)
    place = jnp.where(place, 1.0, 0.0)
    picked = dot(jnp.where(is_token, place, 0.0).astype(bf16), tokens, 1, 0)
    picked = picked + dot(jnp.where(is_token, 0.0, place).astype(bf16), cotangent, 1, 0)
    out_ref[:, :features] = (picked * factor).astype(bf16)

    unit = shard_ref[0] * units + lax.broadcasted_iota(jnp.int32, (units, width), 0)
    choose = unit == lax.broadcasted_iota(jnp.int32, (units, width), 1)
    choose = jnp.where(choose, 1.0, 0.0).astype(bf16)
    for move in moves[4:]:
        move.wait()
    pieces = [
        dot(choose, gate_ref[...], 1, 1),
        dot(choose, up_ref[...], 1, 1),
        dot(choose, down_ref[...], 1, 0),
    ]
    if height > 3 * units:
        pieces.append(jnp.zeros((height - 3 * units, features), f32))
    pieces = jnp.concatenate(pieces, axis=0).astype(bf16)
    for span in range(spans):
        out_ref[span * height : span * height + height, features:] = pieces[
            :, span * 256 : span * 256 + 256
        ]
    used = spans * height
    out_ref[used:, features:] = jnp.zeros((total - used, 256), bf16)


def pack(shard, tokens, cotangent, weight, routed, gate, up, down, experts, size):
    rows, features = tokens.shape
    return pl.pallas_call(
        functools.partial(pack_kernel, size=size),
        out_shape=(
            jax.ShapeDtypeStruct((experts * 8, features + 256), bf16),
            jax.ShapeDtypeStruct((rows, 2 * features), bf16),
            jax.ShapeDtypeStruct((8, 128), jnp.int32),
        ),
        in_specs=[pl.BlockSpec(memory_space=pltpu.SMEM)]
        + [pl.BlockSpec(memory_space=pl.ANY)] * 7,
        out_specs=tuple(in_vmem(3)),
        scratch_shapes=[
            pltpu.VMEM((rows, features), bf16),
            pltpu.VMEM((rows, features), bf16),
            pltpu.VMEM(weight.shape, f32),
            pltpu.VMEM(routed.shape, jnp.int32),
            pltpu.VMEM(gate.shape, bf16),
            pltpu.VMEM(up.shape, bf16),
            pltpu.VMEM(down.shape, bf16),
            pltpu.SemaphoreType.DMA((7,)),
        ],
        compiler_params=pltpu.CompilerParams(vmem_limit_bytes=60 * 2**20),
    )(shard, routed, weight, tokens, cotangent, gate, up, down)


def join_kernel(own_kept, own_came, hot_kept, hot_came, joined_ref, pair_ref):
    own_rows = own_kept.shape[1]
    rows = joined_ref.shape[1] - own_rows
    joined_ref[:, :own_rows, :] = add(own_kept[...], own_came[...])
    hot = add(hot_kept[...], hot_came[...])
    joined_ref[:, own_rows:, :] = hot[:, :rows]
    pair_ref[...] = hot[:, rows:]


def join(own_kept, own_came, hot_kept, hot_came, strip):
    depth, own_rows, _ = own_kept.shape
    rows = own_rows + hot_kept.shape[1] - strip
    return pl.pallas_call(
        join_kernel,
        out_shape=(
            jax.ShapeDtypeStruct((depth, rows, 128), bf16),
            jax.ShapeDtypeStruct((depth, strip, 128), bf16),
        ),
        in_specs=in_vmem(4),
        out_specs=tuple(in_vmem(2)),
        compiler_params=pltpu.CompilerParams(vmem_limit_bytes=48 * 2**20),
    )(own_kept, own_came, hot_kept, hot_came)


def pick_kernel(busiest_ref, piece_ref, out_ref):
    out_ref[...] = jnp.broadcast_to(piece_ref[...], out_ref.shape)


def pick(busiest, arrived, features):
    experts = arrived.shape[0]
    shape = (experts, 8, 256)
    grid_spec = pltpu.PrefetchScalarGridSpec(
        num_scalar_prefetch=1,
        grid=(1,),
        in_specs=[pl.BlockSpec((1, 8, 256), lambda i, chosen: (chosen[0], 0, features // 256))],
        out_specs=pl.BlockSpec(shape, lambda i, chosen: (0, 0, 0)),
    )
    return pl.pallas_call(
        pick_kernel, grid_spec=grid_spec, out_shape=jax.ShapeDtypeStruct(shape, bf16)
    )(busiest, arrived)


def total_kernel(parts_ref, out_ref):
    half = parts_ref.shape[2] - 256
    sums = jnp.sum(parts_ref[:, :, half:].astype(f32), axis=0, keepdims=True).astype(bf16)
    out_ref[...] = jnp.broadcast_to(sums, out_ref.shape)


def total(back):
    return pl.pallas_call(
        total_kernel,
        in_specs=in_vmem(1),
        out_specs=in_vmem(1)[0],
        out_shape=jax.ShapeDtypeStruct((back.shape[0], 8, 256), bf16),
    )(back)


def own_kernel(
    core_ref, rows_ref, gate_ref, up_ref, down_ref, out_ref, kept_ref, passed_ref, grads, down_grads
):
    features, width = gate_ref.shape
    depth = kept_ref.shape[0]
    half = features // 2
    strip = features // (2 * depth)
    units = width // (2 * depth)
    lanes = width // 128
    core = core_ref[0]
    sides = ((kept_ref, core), (passed_ref, 1 - core))
    rows = rows_ref[:, :features]
    down = down_ref[...]
    gate_value = dot(rows, gate_ref[...], 1, 0)
    up_value = dot(rows, up_ref[...], 1, 0)
    upstream = dot(rows, down, 1, 1)
    count = gate_value.shape[0]
    upstream = pltpu.roll(upstream, count - 4, 0)
    sigmoid = jax.nn.sigmoid(gate_value)
    active = gate_value * sigmoid
    slope = sigmoid * (1.0 + gate_value * (1.0 - sigmoid))
    is_token = lax.broadcasted_iota(jnp.int32, (count, width), 0) % 8 < 4
    hidden = jnp.where(is_token, active * up_value, 0.0)
    shifted = pltpu.roll(hidden, 4, 0).astype(bf16)
    hidden = hidden.astype(bf16)
    gate_delta = jnp.where(is_token, upstream * up_value * slope, 0.0).astype(bf16)
    up_delta = jnp.where(is_token, upstream * active, 0.0).astype(bf16)
    for index, delta in enumerate((gate_delta, up_delta)):
        grads[...] = dot(rows, delta, 0, 0)
        for z in range(depth):
            for ref, side in sides:
                start = pl.multiple_of((2 * z + side) * strip, strip)
                block = grads[pl.ds(start, strip), :].astype(bf16)
                for lane in range(lanes):
                    at = (index * lanes + lane) * strip
                    ref[z, at : at + strip, :] = block[:, lane * 128 : lane * 128 + 128]
    down_grads[...] = dot(shifted, rows, 0, 0)
    base = 2 * lanes * strip
    for z in range(depth):
        for ref, side in sides:
            start = pl.multiple_of((2 * z + side) * units, 8)
            block = down_grads[pl.ds(start, units), :]
            for lane in range(0, features // 128, 2):
                at = base + lane * units
                pair = [block[:, i * 128 : i * 128 + 128] for i in (lane, lane + 1)]
                ref[z, at : at + 2 * units, :] = jnp.concatenate(pair, axis=0).astype(bf16)
    output = dot(hidden, down[:, :half], 1, 0) + dot(shifted, down[:, half:], 1, 0)
    out_ref[...] = output.astype(bf16)


def own_expert(core, rows, gate, up, down, depth):
    features, width = gate.shape
    side = jax.ShapeDtypeStruct((depth, 3 * features * width // (2 * depth) // 128, 128), bf16)
    return pl.pallas_call(
        own_kernel,
        out_shape=(jax.ShapeDtypeStruct((rows.shape[0], features // 2), bf16), side, side),
        in_specs=[pl.BlockSpec(memory_space=pltpu.SMEM)] + in_vmem(4),
        out_specs=tuple(in_vmem(3)),
        scratch_shapes=[pltpu.VMEM((features, width), f32), pltpu.VMEM((width, features), f32)],
        compiler_params=pltpu.CompilerParams(vmem_limit_bytes=48 * 2**20),
    )(core, rows, gate, up, down)


def hot_kernel(
    units, core_ref, rows_hbm, blocks_ref, kept_ref, passed_ref, grads_ref, part, pair_part, inputs_ref, scaled_ref, sems
):
    features = part.shape[1]
    depth = kept_ref.shape[0]
    group = part.shape[0] // (2 * depth)
    spans = features // 256
    height = -(-3 * units // 16) * 16
    core = core_ref[0]
    first = pltpu.make_async_copy(rows_hbm.at[:, :features], inputs_ref, sems.at[0])
    second = pltpu.make_async_copy(rows_hbm.at[:, features:], scaled_ref, sems.at[1])
    first.start()
    second.start()
    sliced = jnp.concatenate(
        [blocks_ref[span * height : span * height + height, :] for span in range(spans)], axis=1
    )
    down = sliced[2 * units :]
    first.wait()
    inputs = inputs_ref[...]
    both = dot(sliced[: 2 * units], inputs, 1, 1)
    second.wait()
    scaled = scaled_ref[...]
    upstream = dot(down, scaled, 1, 1)[:units]
    gate_value, up_value = both[:units], both[units:]
    sigmoid = jax.nn.sigmoid(gate_value)
    active = gate_value * sigmoid
    slope = sigmoid * (1.0 + gate_value * (1.0 - sigmoid))
    pair = jnp.concatenate([upstream * up_value * slope, upstream * active], axis=0)
    spare = jnp.zeros((height - 3 * units, gate_value.shape[1]), f32)
    hidden = active * up_value
    if spare.shape[0]:
        hidden = jnp.concatenate([hidden, spare], axis=0)
    hidden = hidden.astype(bf16)
    part[...] = dot(hidden, down, 0, 0)
    empty = jnp.zeros_like(pair)
    spread = [jnp.where(core == 0, pair, empty), jnp.where(core == 1, pair, empty)]
    if 4 * units < 128:
        spread.append(jnp.zeros((128 - 4 * units, pair.shape[1]), f32))
    spread = jnp.concatenate(spread, axis=0).astype(bf16)
    pair_part[...] = dot(inputs, spread, 0, 1)
    strip = features // (2 * depth)
    wide = group * (features // 128)
    for z in range(depth):
        for ref, side in ((kept_ref, core), (passed_ref, 1 - core)):
            start = pl.multiple_of((2 * z + side) * group, group)
            block = part[pl.ds(start, group), :].astype(bf16)
            for lane in range(features // 128):
                ref[z, lane * group : lane * group + group, :] = block[
                    :, lane * 128 : lane * 128 + 128
                ]
            start = pl.multiple_of((2 * z + side) * strip, strip)
            ref[z, wide:, :] = pair_part[pl.ds(start, strip), :].astype(bf16)
    grads = dot(hidden, scaled, 1, 0)[:units]
    for lane in range(0, features // 128, 2):
        both = [grads[:, i * 128 : i * 128 + 128] for i in (lane, lane + 1)]
        grads_ref[lane * units : (lane + 2) * units, :] = jnp.concatenate(both, 0).astype(bf16)
    used = features // 128 * units
    grads_ref[used:, :] = jnp.zeros((grads_ref.shape[0] - used, 128), bf16)


def hot_expert(core, gathered, blocks, units, depth):
    total, features = gathered.shape[0], gathered.shape[1] // 2
    height = total // (2 * depth) * features // 128 + features // (2 * depth)
    side = jax.ShapeDtypeStruct((depth, height, 128), bf16)
    return pl.pallas_call(
        functools.partial(hot_kernel, units),
        out_shape=(side, side, jax.ShapeDtypeStruct((blocks.shape[0], 128), bf16)),
        in_specs=[pl.BlockSpec(memory_space=pltpu.SMEM), pl.BlockSpec(memory_space=pl.ANY)]
        + in_vmem(1),
        out_specs=tuple(in_vmem(3)),
        scratch_shapes=[
            pltpu.VMEM((total, features), f32),
            pltpu.VMEM((features, 128), f32),
            pltpu.VMEM((total, features), bf16),
            pltpu.VMEM((total, features), bf16),
            pltpu.SemaphoreType.DMA((2,)),
        ],
        compiler_params=pltpu.CompilerParams(vmem_limit_bytes=59 * 2**20),
    )(core, gathered, blocks)


def middle_kernel(
    units, routed_ref, weight_ref, cotangent_ref, back_ref, summed_ref,
    layer_ref, route_ref, gate_ref, up_ref, down_ref, spread_ref
):
    rows, features = cotangent_ref.shape
    half = features // 2
    strip, width = gate_ref.shape
    experts = back_ref.shape[0] // 8
    hot_weight, busiest, place, is_token, spots = tables(routed_ref, weight_ref, experts)
    cotangent = cotangent_ref[...]
    results = back_ref[:, :half]
    own_rows = summed_ref.shape[0] - rows * (features // 128)
    blocks = [
        summed_ref[own_rows + i * rows : own_rows + (i + 1) * rows, :]
        for i in range(features // 128)
    ]
    hot_out = jnp.concatenate(blocks, axis=1).astype(f32)
    sides = []
    for side in (jnp.where(is_token, spots, 0.0), jnp.where(is_token, 0.0, spots)):
        high = side.astype(bf16)
        low = (side - high.astype(f32)).astype(bf16)
        sides.append(dot(high, results, 0, 0) + dot(low, results, 0, 0))
    layer = jnp.concatenate(sides, axis=1) + hot_weight * hot_out
    layer_ref[...] = layer.astype(bf16)

    left = dot(results, cotangent[:, :half], 1, 1)
    right = dot(results, cotangent[:, half:], 1, 1)
    products = jnp.where(place, jnp.where(is_token, left, right), 0.0)
    hot_column = jnp.sum(hot_out * cotangent.astype(f32), axis=1, keepdims=True)
    first = lax.broadcasted_iota(jnp.int32, (rows, rows), 0)
    second = lax.broadcasted_iota(jnp.int32, (rows, rows), 1)
    hot_row = jnp.sum(jnp.where(first == second, hot_column, 0.0), axis=0, keepdims=True)
    owner = lax.broadcasted_iota(jnp.int32, products.shape, 0) // 8
    for k in range(routed_ref.shape[0]):
        named = routed_ref[k : k + 1, :]
        cold = jnp.sum(jnp.where(owner == named, products, 0.0), axis=0, keepdims=True)
        route_ref[k : k + 1, :] = cold + jnp.where(named == busiest, hot_row, 0.0)

    lanes = width // 128
    for index, ref in enumerate((gate_ref, up_ref)):
        for lane in range(lanes):
            at = (index * lanes + lane) * strip
            ref[:, lane * 128 : lane * 128 + 128] = summed_ref[at : at + strip, :].astype(f32)
    base = 2 * lanes * strip
    unpair(down_ref, summed_ref, base, 0, units)

    shape = (spread_ref.shape[0], 2 * width)
    lane = lax.broadcasted_iota(jnp.int32, (shape[0], 1), 0)
    within = lane % 128
    column = (within % (2 * units)) // units * width + within % units
    column = column + (lane // 128 * 2 + within // (2 * units)) * units
    column = jnp.where(within < 4 * units, column, -1)
    match = lax.broadcasted_iota(jnp.int32, shape, 1) == column
    spread_ref[...] = jnp.where(match, 1.0, 0.0).astype(bf16)


def unpair(out_ref, from_ref, base, lane_base, units):
    for lane in range(0, out_ref.shape[1] // 128, 2):
        at = base + lane * units
        pair = from_ref[at : at + 2 * units, lane_base : lane_base + 128].astype(f32)
        out_ref[:, lane * 128 : lane * 128 + 128] = pair[:units]
        out_ref[:, lane * 128 + 128 : lane * 128 + 256] = pair[units:]


def middle(routed, weight, cotangent, back, summed, units, strip, depth):
    rows, features = cotangent.shape
    width = units * 2 * depth
    return pl.pallas_call(
        functools.partial(middle_kernel, units),
        out_shape=(
            jax.ShapeDtypeStruct((rows, features), bf16),
            jax.ShapeDtypeStruct(weight.shape, f32),
            jax.ShapeDtypeStruct((strip, width), f32),
            jax.ShapeDtypeStruct((strip, width), f32),
            jax.ShapeDtypeStruct((units, features), f32),
            jax.ShapeDtypeStruct((depth * 128, 2 * width), bf16),
        ),
        in_specs=in_vmem(5),
        out_specs=tuple(in_vmem(6)),
        compiler_params=pltpu.CompilerParams(vmem_limit_bytes=48 * 2**20),
    )(routed, weight, cotangent, back, summed)


def last_kernel(
    units, home_ref, blocks_ref, gate_ref, up_ref, down_ref, spread_ref,
    gate_out, up_out, down_out, scratch
):
    strip, width = gate_ref.shape
    depth = spread_ref.shape[0] // 128
    home = home_ref[0] == 1
    blocks = [blocks_ref[z * strip : (z + 1) * strip, :128] for z in range(depth)]
    pair = dot(jnp.concatenate(blocks, axis=1), spread_ref[...], 1, 0)
    gate_out[...] = gate_ref[...] + jnp.where(home, pair[:, :width], 0.0)
    up_out[...] = up_ref[...] + jnp.where(home, pair[:, width:], 0.0)
    unpair(scratch, blocks_ref, 0, 128, units)
    down_out[...] = down_ref[...] + jnp.where(home, scratch[...], 0.0)


def last(home, blocks, gate, up, down, spread):
    units = down.shape[0]
    return pl.pallas_call(
        functools.partial(last_kernel, units),
        out_shape=tuple(jax.ShapeDtypeStruct(x.shape, f32) for x in (gate, up, down)),
        in_specs=[pl.BlockSpec(memory_space=pltpu.SMEM)] + in_vmem(5),
        out_specs=tuple(in_vmem(3)),
        scratch_shapes=[pltpu.VMEM(down.shape, f32)],
        compiler_params=pltpu.CompilerParams(vmem_limit_bytes=48 * 2**20),
    )(home, blocks, gate, up, down, spread)


def on_device(
    tokens, cotangent, route_weight, routed_experts, gate_weights, up_weights, down_weights
):
    experts = lax.axis_size("expert")
    size = lax.axis_size("dp")
    depth = size // 2
    mine = lax.axis_index("expert")
    shard = lax.axis_index("dp")
    core = shard % 2
    core_word = core.astype(jnp.int32).reshape(1)
    rows, features = tokens.shape
    half = features // 2
    gate, up, down = gate_weights[0], up_weights[0], down_weights[0]
    width = gate.shape[1]
    units = width // size
    strip = features // size

    shard_word = shard.astype(jnp.int32).reshape(1)
    outgoing, hot_rows, found = pack(
        shard_word,
        tokens,
        cotangent,
        route_weight.T,
        routed_experts.T,
        gate,
        up,
        down,
        experts,
        size,
    )
    gathered = lax.all_gather(hot_rows, "dp", axis=0, tiled=True)
    arrived = plane_exchange(outgoing.reshape(experts, 8, features + 256))
    picked = pick(found[0, :1], arrived, features)
    arrived, picked, routed, weight = lax.optimization_barrier(
        (arrived, picked, routed_experts.T, route_weight.T)
    )
    blocks = plane_exchange(picked)
    returning, own_kept, own_passed = own_expert(
        core_word, arrived.reshape(experts * 8, features + 256), gate, up, down, depth
    )
    blocks, own_passed = lax.optimization_barrier((blocks, own_passed))
    own_came = core_swap(own_passed)
    hot_kept, hot_passed, hot_grads = hot_expert(
        core_word, gathered, blocks.reshape(experts * 8, 256), units, depth
    )
    hot_came = core_swap(hot_passed)
    joined, pair = join(own_kept, own_came, hot_kept, hot_came, strip)
    summed = z_reduce_scatter(joined)[0]
    pair = pad_blocks(z_exchange(pair).reshape(depth * strip // 8, 8, 128), experts)

    back = plane_exchange(
        jnp.concatenate(
            [returning.reshape(experts, 8, half), pair, hot_grads.reshape(experts, 8, 128)], axis=2
        )
    )
    hot_blocks = plane_exchange(total(back))
    layer_out, route_gradient, own_gate, own_up, own_down, spread = middle(
        routed, weight, cotangent, back.reshape(experts * 8, -1), summed, units, strip, depth
    )
    home = (mine == found[0, 0]).astype(jnp.int32).reshape(1)
    gate_gradient, up_gradient, down_gradient = last(
        home, hot_blocks.reshape(experts * 8, 256), own_gate, own_up, own_down, spread
    )
    return (
        layer_out,
        route_gradient.T,
        gate_gradient[None],
        up_gradient[None],
        down_gradient[None],
    )


def solution(mesh):
    in_specs = (
        P(("dp", "expert"), None),
        P(("dp", "expert"), None),
        P(("dp", "expert"), None),
        P(("dp", "expert"), None),
        P("expert", None, None),
        P("expert", None, None),
        P("expert", None, None),
    )
    out_specs = (
        P(("dp", "expert"), None),
        P(("dp", "expert"), None),
        P("expert", "dp", None),
        P("expert", "dp", None),
        P("expert", "dp", None),
    )
    return jax.shard_map(
        on_device, mesh=mesh, in_specs=in_specs, out_specs=out_specs, check_vma=False
    )
```

```python
import functools

import jax
import jax.numpy as jnp
from jax import lax
from jax.experimental import pallas as pl
from jax.experimental.pallas import tpu as pltpu
from jax.sharding import PartitionSpec as P

f32 = jnp.float32
bf16 = jnp.bfloat16
highest = lax.Precision.HIGHEST


def dot(lhs, rhs, lhs_dim, rhs_dim, precision=None):
    dims = (((lhs_dim,), (rhs_dim,)), ((), ()))
    return lax.dot_general(lhs, rhs, dims, precision=precision, preferred_element_type=f32)


def plane_exchange(blocks):
    return lax.all_to_all(blocks, "expert", split_axis=0, concat_axis=0, tiled=True)


def core_swap(block):
    size = lax.axis_size("dp")
    return lax.ppermute(block, "dp", [(i, i ^ 1) for i in range(size)])


def z_exchange(blocks):
    size = lax.axis_size("dp")
    groups = [list(range(core, size, 2)) for core in range(2)]
    return lax.all_to_all(
        blocks, "dp", split_axis=0, concat_axis=0, tiled=True, axis_index_groups=groups
    )


def z_reduce_scatter(blocks):
    size = lax.axis_size("dp")
    groups = [list(range(core, size, 2)) for core in range(2)]
    return lax.psum_scatter(
        blocks, "dp", scatter_dimension=0, tiled=True, axis_index_groups=groups
    )


def add(one, other):
    return (one.astype(f32) + other.astype(f32)).astype(bf16)


def pad_blocks(blocks, count):
    return jnp.pad(blocks, ((0, count - blocks.shape[0]),) + ((0, 0),) * (blocks.ndim - 1))


def in_vmem(count):
    return [pl.BlockSpec(memory_space=pltpu.VMEM)] * count


def tables(routed_ref, weight_ref, experts):
    rows = routed_ref.shape[1]
    total = experts * 8
    names = lax.broadcasted_iota(jnp.int32, (experts, rows), 0)
    named = jnp.zeros((experts, rows), f32)
    table = jnp.zeros((experts, rows), f32)
    for k in range(routed_ref.shape[0]):
        hit = routed_ref[k : k + 1, :] == names
        named = jnp.where(hit, 1.0, named)
        table = jnp.where(hit, weight_ref[k : k + 1, :], table)
    counts = jnp.sum(named, axis=1, keepdims=True)
    busy = counts == jnp.max(counts, axis=0, keepdims=True)
    busiest = jnp.max(jnp.where(busy, names, 0)[:, :1], axis=0, keepdims=True)
    cold = jnp.where(busy, 0.0, named)
    first = lax.broadcasted_iota(jnp.int32, (rows, rows), 0)
    second = lax.broadcasted_iota(jnp.int32, (rows, rows), 1)
    before = jnp.where(first < second, 1.0, 0.0)
    rank = dot(cold.astype(bf16), before.astype(bf16), 1, 0)
    code = jnp.where(cold > 0.0, rank + 1.0, 0.0)
    hot_row = jnp.sum(jnp.where(busy, table, 0.0), axis=0, keepdims=True)
    hot_weight = jnp.sum(jnp.where(first == second, hot_row, 0.0), axis=1, keepdims=True)
    owner = lax.broadcasted_iota(jnp.int32, (total, experts), 0) // 8
    spread = owner == lax.broadcasted_iota(jnp.int32, (total, experts), 1)
    spread = jnp.where(spread, 1.0, 0.0)
    code = dot(spread.astype(bf16), code.astype(bf16), 1, 0)
    table = dot(spread, table, 1, 0, highest)
    row = lax.broadcasted_iota(jnp.int32, (total, rows), 0)
    is_token = row % 8 < 4
    place = code == (row % 4 + 1).astype(f32)
    return hot_weight, busiest, place, is_token, jnp.where(place, table, 0.0)


def pack_kernel(
    shard_ref, routed_hbm, weight_hbm, tokens_hbm, cotangent_hbm, gate_hbm, up_hbm, down_hbm, out_ref, hot_ref, busiest_ref,
    tokens_ref, cotangent_ref, weight_ref, routed_ref, gate_ref, up_ref, down_ref, sems, size
):
    moves = []
    sources = (routed_hbm, weight_hbm, tokens_hbm, cotangent_hbm, gate_hbm, up_hbm, down_hbm)
    targets = (routed_ref, weight_ref, tokens_ref, cotangent_ref, gate_ref, up_ref, down_ref)
    for index, (source, target) in enumerate(zip(sources, targets)):
        moves.append(pltpu.make_async_copy(source, target, sems.at[index]))
        moves[index].start()
    rows, features = tokens_ref.shape
    width = gate_ref.shape[1]
    units = width // size
    height, spans = -(-3 * units // 16) * 16, features // 256
    total = out_ref.shape[0]
    experts = total // 8
    moves[0].wait()
    moves[1].wait()
    hot_weight, busiest, place, is_token, spots = tables(routed_ref, weight_ref, experts)
    busiest_ref[...] = jnp.broadcast_to(busiest, busiest_ref.shape)
    moves[2].wait()
    moves[3].wait()
    tokens = tokens_ref[...]
    cotangent = cotangent_ref[...]
    hot_ref[:, :features] = tokens
    hot_ref[:, features:] = (hot_weight * cotangent.astype(f32)).astype(bf16)

    slot_weight = jnp.sum(spots, axis=1, keepdims=True)
    factor = jnp.where(is_token[:, :1], 1.0, slot_weight)
    place = jnp.where(place, 1.0, 0.0)
    picked = dot(jnp.where(is_token, place, 0.0).astype(bf16), tokens, 1, 0)
    picked = picked + dot(jnp.where(is_token, 0.0, place).astype(bf16), cotangent, 1, 0)
    out_ref[:, :features] = (picked * factor).astype(bf16)

    unit = shard_ref[0] * units + lax.broadcasted_iota(jnp.int32, (units, width), 0)
    choose = unit == lax.broadcasted_iota(jnp.int32, (units, width), 1)
    choose = jnp.where(choose, 1.0, 0.0).astype(bf16)
    for move in moves[4:]:
        move.wait()
    pieces = [
        dot(choose, gate_ref[...], 1, 1),
        dot(choose, up_ref[...], 1, 1),
        dot(choose, down_ref[...], 1, 0),
    ]
    if height > 3 * units:
        pieces.append(jnp.zeros((height - 3 * units, features), f32))
    pieces = jnp.concatenate(pieces, axis=0).astype(bf16)
    for span in range(spans):
        out_ref[span * height : span * height + height, features:] = pieces[
            :, span * 256 : span * 256 + 256
        ]
    used = spans * height
    out_ref[used:, features:] = jnp.zeros((total - used, 256), bf16)


def pack(shard, tokens, cotangent, weight, routed, gate, up, down, experts, size):
    rows, features = tokens.shape
    return pl.pallas_call(
        functools.partial(pack_kernel, size=size),
        out_shape=(
            jax.ShapeDtypeStruct((experts * 8, features + 256), bf16),
            jax.ShapeDtypeStruct((rows, 2 * features), bf16),
            jax.ShapeDtypeStruct((8, 128), jnp.int32),
        ),
        in_specs=[pl.BlockSpec(memory_space=pltpu.SMEM)]
        + [pl.BlockSpec(memory_space=pl.ANY)] * 7,
        out_specs=tuple(in_vmem(3)),
        scratch_shapes=[
            pltpu.VMEM((rows, features), bf16),
            pltpu.VMEM((rows, features), bf16),
            pltpu.VMEM(weight.shape, f32),
            pltpu.VMEM(routed.shape, jnp.int32),
            pltpu.VMEM(gate.shape, bf16),
            pltpu.VMEM(up.shape, bf16),
            pltpu.VMEM(down.shape, bf16),
            pltpu.SemaphoreType.DMA((7,)),
        ],
        compiler_params=pltpu.CompilerParams(vmem_limit_bytes=60 * 2**20),
    )(shard, routed, weight, tokens, cotangent, gate, up, down)


def join_kernel(own_kept, own_came, hot_kept, hot_came, joined_ref, pair_ref):
    own_rows = own_kept.shape[1]
    rows = joined_ref.shape[1] - own_rows
    joined_ref[:, :own_rows, :] = add(own_kept[...], own_came[...])
    hot = add(hot_kept[...], hot_came[...])
    joined_ref[:, own_rows:, :] = hot[:, :rows]
    pair_ref[...] = hot[:, rows:]


def join(own_kept, own_came, hot_kept, hot_came, strip):
    depth, own_rows, _ = own_kept.shape
    rows = own_rows + hot_kept.shape[1] - strip
    return pl.pallas_call(
        join_kernel,
        out_shape=(
            jax.ShapeDtypeStruct((depth, rows, 128), bf16),
            jax.ShapeDtypeStruct((depth, strip, 128), bf16),
        ),
        in_specs=in_vmem(4),
        out_specs=tuple(in_vmem(2)),
        compiler_params=pltpu.CompilerParams(vmem_limit_bytes=48 * 2**20),
    )(own_kept, own_came, hot_kept, hot_came)


def pick_kernel(busiest_ref, piece_ref, out_ref):
    out_ref[...] = jnp.broadcast_to(piece_ref[...], out_ref.shape)


def pick(busiest, arrived, features):
    experts = arrived.shape[0]
    shape = (experts, 8, 256)
    grid_spec = pltpu.PrefetchScalarGridSpec(
        num_scalar_prefetch=1,
        grid=(1,),
        in_specs=[pl.BlockSpec((1, 8, 256), lambda i, chosen: (chosen[0], 0, features // 256))],
        out_specs=pl.BlockSpec(shape, lambda i, chosen: (0, 0, 0)),
    )
    return pl.pallas_call(
        pick_kernel, grid_spec=grid_spec, out_shape=jax.ShapeDtypeStruct(shape, bf16)
    )(busiest, arrived)


def total_kernel(parts_ref, out_ref):
    half = parts_ref.shape[2] - 256
    sums = jnp.sum(parts_ref[:, :, half:].astype(f32), axis=0, keepdims=True).astype(bf16)
    out_ref[...] = jnp.broadcast_to(sums, out_ref.shape)


def total(back):
    return pl.pallas_call(
        total_kernel,
        in_specs=in_vmem(1),
        out_specs=in_vmem(1)[0],
        out_shape=jax.ShapeDtypeStruct((back.shape[0], 8, 256), bf16),
    )(back)


def own_kernel(
    core_ref, rows_ref, gate_ref, up_ref, down_ref, out_ref, kept_ref, passed_ref, grads, down_grads
):
    features, width = gate_ref.shape
    depth = kept_ref.shape[0]
    half = features // 2
    strip = features // (2 * depth)
    units = width // (2 * depth)
    lanes = width // 128
    core = core_ref[0]
    sides = ((kept_ref, core), (passed_ref, 1 - core))
    rows = rows_ref[:, :features]
    down = down_ref[...]
    gate_value = dot(rows, gate_ref[...], 1, 0)
    up_value = dot(rows, up_ref[...], 1, 0)
    upstream = dot(rows, down, 1, 1)
    count = gate_value.shape[0]
    upstream = pltpu.roll(upstream, count - 4, 0)
    sigmoid = jax.nn.sigmoid(gate_value)
    active = gate_value * sigmoid
    slope = sigmoid * (1.0 + gate_value * (1.0 - sigmoid))
    is_token = lax.broadcasted_iota(jnp.int32, (count, width), 0) % 8 < 4
    hidden = jnp.where(is_token, active * up_value, 0.0)
    shifted = pltpu.roll(hidden, 4, 0).astype(bf16)
    hidden = hidden.astype(bf16)
    gate_delta = jnp.where(is_token, upstream * up_value * slope, 0.0).astype(bf16)
    up_delta = jnp.where(is_token, upstream * active, 0.0).astype(bf16)
    for index, delta in enumerate((gate_delta, up_delta)):
        grads[...] = dot(rows, delta, 0, 0)
        for z in range(depth):
            for ref, side in sides:
                start = pl.multiple_of((2 * z + side) * strip, strip)
                block = grads[pl.ds(start, strip), :].astype(bf16)
                for lane in range(lanes):
                    at = (index * lanes + lane) * strip
                    ref[z, at : at + strip, :] = block[:, lane * 128 : lane * 128 + 128]
    down_grads[...] = dot(shifted, rows, 0, 0)
    base = 2 * lanes * strip
    for z in range(depth):
        for ref, side in sides:
            start = pl.multiple_of((2 * z + side) * units, 8)
            block = down_grads[pl.ds(start, units), :]
            for lane in range(0, features // 128, 2):
                at = base + lane * units
                pair = [block[:, i * 128 : i * 128 + 128] for i in (lane, lane + 1)]
                ref[z, at : at + 2 * units, :] = jnp.concatenate(pair, axis=0).astype(bf16)
    output = dot(hidden, down[:, :half], 1, 0) + dot(shifted, down[:, half:], 1, 0)
    out_ref[...] = output.astype(bf16)


def own_expert(core, rows, gate, up, down, depth):
    features, width = gate.shape
    side = jax.ShapeDtypeStruct((depth, 3 * features * width // (2 * depth) // 128, 128), bf16)
    return pl.pallas_call(
        own_kernel,
        out_shape=(jax.ShapeDtypeStruct((rows.shape[0], features // 2), bf16), side, side),
        in_specs=[pl.BlockSpec(memory_space=pltpu.SMEM)] + in_vmem(4),
        out_specs=tuple(in_vmem(3)),
        scratch_shapes=[pltpu.VMEM((features, width), f32), pltpu.VMEM((width, features), f32)],
        compiler_params=pltpu.CompilerParams(vmem_limit_bytes=48 * 2**20),
    )(core, rows, gate, up, down)


def hot_kernel(
    units, core_ref, rows_hbm, blocks_ref, kept_ref, passed_ref, grads_ref, part, pair_part, inputs_ref, scaled_ref, sems
):
    features = part.shape[1]
    depth = kept_ref.shape[0]
    group = part.shape[0] // (2 * depth)
    spans = features // 256
    height = -(-3 * units // 16) * 16
    core = core_ref[0]
    first = pltpu.make_async_copy(rows_hbm.at[:, :features], inputs_ref, sems.at[0])
    second = pltpu.make_async_copy(rows_hbm.at[:, features:], scaled_ref, sems.at[1])
    first.start()
    second.start()
    sliced = jnp.concatenate(
        [blocks_ref[span * height : span * height + height, :] for span in range(spans)], axis=1
    )
    down = sliced[2 * units :]
    first.wait()
    inputs = inputs_ref[...]
    both = dot(sliced[: 2 * units], inputs, 1, 1)
    second.wait()
    scaled = scaled_ref[...]
    upstream = dot(down, scaled, 1, 1)[:units]
    gate_value, up_value = both[:units], both[units:]
    sigmoid = jax.nn.sigmoid(gate_value)
    active = gate_value * sigmoid
    slope = sigmoid * (1.0 + gate_value * (1.0 - sigmoid))
    pair = jnp.concatenate([upstream * up_value * slope, upstream * active], axis=0)
    spare = jnp.zeros((height - 3 * units, gate_value.shape[1]), f32)
    hidden = active * up_value
    if spare.shape[0]:
        hidden = jnp.concatenate([hidden, spare], axis=0)
    hidden = hidden.astype(bf16)
    part[...] = dot(hidden, down, 0, 0)
    empty = jnp.zeros_like(pair)
    spread = [jnp.where(core == 0, pair, empty), jnp.where(core == 1, pair, empty)]
    if 4 * units < 128:
        spread.append(jnp.zeros((128 - 4 * units, pair.shape[1]), f32))
    spread = jnp.concatenate(spread, axis=0).astype(bf16)
    pair_part[...] = dot(inputs, spread, 0, 1)
    strip = features // (2 * depth)
    wide = group * (features // 128)
    for z in range(depth):
        for ref, side in ((kept_ref, core), (passed_ref, 1 - core)):
            start = pl.multiple_of((2 * z + side) * group, group)
            block = part[pl.ds(start, group), :].astype(bf16)
            for lane in range(features // 128):
                ref[z, lane * group : lane * group + group, :] = block[
                    :, lane * 128 : lane * 128 + 128
                ]
            start = pl.multiple_of((2 * z + side) * strip, strip)
            ref[z, wide:, :] = pair_part[pl.ds(start, strip), :].astype(bf16)
    grads = dot(hidden, scaled, 1, 0)[:units]
    for lane in range(0, features // 128, 2):
        both = [grads[:, i * 128 : i * 128 + 128] for i in (lane, lane + 1)]
        grads_ref[lane * units : (lane + 2) * units, :] = jnp.concatenate(both, 0).astype(bf16)
    used = features // 128 * units
    grads_ref[used:, :] = jnp.zeros((grads_ref.shape[0] - used, 128), bf16)


def hot_expert(core, gathered, blocks, units, depth):
    total, features = gathered.shape[0], gathered.shape[1] // 2
    height = total // (2 * depth) * features // 128 + features // (2 * depth)
    side = jax.ShapeDtypeStruct((depth, height, 128), bf16)
    return pl.pallas_call(
        functools.partial(hot_kernel, units),
        out_shape=(side, side, jax.ShapeDtypeStruct((blocks.shape[0], 128), bf16)),
        in_specs=[pl.BlockSpec(memory_space=pltpu.SMEM), pl.BlockSpec(memory_space=pl.ANY)]
        + in_vmem(1),
        out_specs=tuple(in_vmem(3)),
        scratch_shapes=[
            pltpu.VMEM((total, features), f32),
            pltpu.VMEM((features, 128), f32),
            pltpu.VMEM((total, features), bf16),
            pltpu.VMEM((total, features), bf16),
            pltpu.SemaphoreType.DMA((2,)),
        ],
        compiler_params=pltpu.CompilerParams(vmem_limit_bytes=48 * 2**20),
    )(core, gathered, blocks)


def middle_kernel(
    units, routed_ref, weight_ref, cotangent_ref, back_ref, summed_ref,
    layer_ref, route_ref, gate_ref, up_ref, down_ref, spread_ref
):
    rows, features = cotangent_ref.shape
    half = features // 2
    strip, width = gate_ref.shape
    experts = back_ref.shape[0] // 8
    hot_weight, busiest, place, is_token, spots = tables(routed_ref, weight_ref, experts)
    cotangent = cotangent_ref[...]
    results = back_ref[:, :half]
    own_rows = summed_ref.shape[0] - rows * (features // 128)
    blocks = [
        summed_ref[own_rows + i * rows : own_rows + (i + 1) * rows, :]
        for i in range(features // 128)
    ]
    hot_out = jnp.concatenate(blocks, axis=1).astype(f32)
    sides = []
    for side in (jnp.where(is_token, spots, 0.0), jnp.where(is_token, 0.0, spots)):
        high = side.astype(bf16)
        low = (side - high.astype(f32)).astype(bf16)
        sides.append(dot(high, results, 0, 0) + dot(low, results, 0, 0))
    layer = jnp.concatenate(sides, axis=1) + hot_weight * hot_out
    layer_ref[...] = layer.astype(bf16)

    left = dot(results, cotangent[:, :half], 1, 1)
    right = dot(results, cotangent[:, half:], 1, 1)
    products = jnp.where(place, jnp.where(is_token, left, right), 0.0)
    hot_column = jnp.sum(hot_out * cotangent.astype(f32), axis=1, keepdims=True)
    first = lax.broadcasted_iota(jnp.int32, (rows, rows), 0)
    second = lax.broadcasted_iota(jnp.int32, (rows, rows), 1)
    hot_row = jnp.sum(jnp.where(first == second, hot_column, 0.0), axis=0, keepdims=True)
    owner = lax.broadcasted_iota(jnp.int32, products.shape, 0) // 8
    for k in range(routed_ref.shape[0]):
        named = routed_ref[k : k + 1, :]
        cold = jnp.sum(jnp.where(owner == named, products, 0.0), axis=0, keepdims=True)
        route_ref[k : k + 1, :] = cold + jnp.where(named == busiest, hot_row, 0.0)

    lanes = width // 128
    for index, ref in enumerate((gate_ref, up_ref)):
        for lane in range(lanes):
            at = (index * lanes + lane) * strip
            ref[:, lane * 128 : lane * 128 + 128] = summed_ref[at : at + strip, :].astype(f32)
    base = 2 * lanes * strip
    unpair(down_ref, summed_ref, base, 0, units)

    shape = (spread_ref.shape[0], 2 * width)
    lane = lax.broadcasted_iota(jnp.int32, (shape[0], 1), 0)
    within = lane % 128
    column = (within % (2 * units)) // units * width + within % units
    column = column + (lane // 128 * 2 + within // (2 * units)) * units
    column = jnp.where(within < 4 * units, column, -1)
    match = lax.broadcasted_iota(jnp.int32, shape, 1) == column
    spread_ref[...] = jnp.where(match, 1.0, 0.0).astype(bf16)


def unpair(out_ref, from_ref, base, lane_base, units):
    for lane in range(0, out_ref.shape[1] // 128, 2):
        at = base + lane * units
        pair = from_ref[at : at + 2 * units, lane_base : lane_base + 128].astype(f32)
        out_ref[:, lane * 128 : lane * 128 + 128] = pair[:units]
        out_ref[:, lane * 128 + 128 : lane * 128 + 256] = pair[units:]


def middle(routed, weight, cotangent, back, summed, units, strip, depth):
    rows, features = cotangent.shape
    width = units * 2 * depth
    return pl.pallas_call(
        functools.partial(middle_kernel, units),
        out_shape=(
            jax.ShapeDtypeStruct((rows, features), bf16),
            jax.ShapeDtypeStruct(weight.shape, f32),
            jax.ShapeDtypeStruct((strip, width), f32),
            jax.ShapeDtypeStruct((strip, width), f32),
            jax.ShapeDtypeStruct((units, features), f32),
            jax.ShapeDtypeStruct((depth * 128, 2 * width), bf16),
        ),
        in_specs=in_vmem(5),
        out_specs=tuple(in_vmem(6)),
        compiler_params=pltpu.CompilerParams(vmem_limit_bytes=48 * 2**20),
    )(routed, weight, cotangent, back, summed)


def last_kernel(
    units, home_ref, blocks_ref, gate_ref, up_ref, down_ref, spread_ref,
    gate_out, up_out, down_out, scratch
):
    strip, width = gate_ref.shape
    depth = spread_ref.shape[0] // 128
    home = home_ref[0] == 1
    blocks = [blocks_ref[z * strip : (z + 1) * strip, :128] for z in range(depth)]
    pair = dot(jnp.concatenate(blocks, axis=1), spread_ref[...], 1, 0)
    gate_out[...] = gate_ref[...] + jnp.where(home, pair[:, :width], 0.0)
    up_out[...] = up_ref[...] + jnp.where(home, pair[:, width:], 0.0)
    unpair(scratch, blocks_ref, 0, 128, units)
    down_out[...] = down_ref[...] + jnp.where(home, scratch[...], 0.0)


def last(home, blocks, gate, up, down, spread):
    units = down.shape[0]
    return pl.pallas_call(
        functools.partial(last_kernel, units),
        out_shape=tuple(jax.ShapeDtypeStruct(x.shape, f32) for x in (gate, up, down)),
        in_specs=[pl.BlockSpec(memory_space=pltpu.SMEM)] + in_vmem(5),
        out_specs=tuple(in_vmem(3)),
        scratch_shapes=[pltpu.VMEM(down.shape, f32)],
        compiler_params=pltpu.CompilerParams(vmem_limit_bytes=48 * 2**20),
    )(home, blocks, gate, up, down, spread)


def on_device(
    tokens, cotangent, route_weight, routed_experts, gate_weights, up_weights, down_weights
):
    experts = lax.axis_size("expert")
    size = lax.axis_size("dp")
    depth = size // 2
    mine = lax.axis_index("expert")
    shard = lax.axis_index("dp")
    core = shard % 2
    core_word = core.astype(jnp.int32).reshape(1)
    rows, features = tokens.shape
    half = features // 2
    gate, up, down = gate_weights[0], up_weights[0], down_weights[0]
    width = gate.shape[1]
    units = width // size
    strip = features // size

    shard_word = shard.astype(jnp.int32).reshape(1)
    outgoing, hot_rows, found = pack(
        shard_word,
        tokens,
        cotangent,
        route_weight.T,
        routed_experts.T,
        gate,
        up,
        down,
        experts,
        size,
    )
    gathered = lax.all_gather(hot_rows, "dp", axis=0, tiled=True)
    arrived = plane_exchange(outgoing.reshape(experts, 8, features + 256))
    picked = pick(found[0, :1], arrived, features)
    arrived, picked, routed, weight = lax.optimization_barrier(
        (arrived, picked, routed_experts.T, route_weight.T)
    )
    blocks = plane_exchange(picked)
    returning, own_kept, own_passed = own_expert(
        core_word, arrived.reshape(experts * 8, features + 256), gate, up, down, depth
    )
    blocks, own_passed = lax.optimization_barrier((blocks, own_passed))
    own_came = core_swap(own_passed)
    hot_kept, hot_passed, hot_grads = hot_expert(
        core_word, gathered, blocks.reshape(experts * 8, 256), units, depth
    )
    hot_came = core_swap(hot_passed)
    joined, pair = join(own_kept, own_came, hot_kept, hot_came, strip)
    summed = z_reduce_scatter(joined)[0]
    pair = pad_blocks(z_exchange(pair).reshape(depth * strip // 8, 8, 128), experts)

    back = plane_exchange(
        jnp.concatenate(
            [returning.reshape(experts, 8, half), pair, hot_grads.reshape(experts, 8, 128)], axis=2
        )
    )
    hot_blocks = plane_exchange(total(back))
    layer_out, route_gradient, own_gate, own_up, own_down, spread = middle(
        routed, weight, cotangent, back.reshape(experts * 8, -1), summed, units, strip, depth
    )
    home = (mine == found[0, 0]).astype(jnp.int32).reshape(1)
    gate_gradient, up_gradient, down_gradient = last(
        home, hot_blocks.reshape(experts * 8, 256), own_gate, own_up, own_down, spread
    )
    return (
        layer_out,
        route_gradient.T,
        gate_gradient[None],
        up_gradient[None],
        down_gradient[None],
    )


def solution(mesh):
    in_specs = (
        P(("dp", "expert"), None),
        P(("dp", "expert"), None),
        P(("dp", "expert"), None),
        P(("dp", "expert"), None),
        P("expert", None, None),
        P("expert", None, None),
        P("expert", None, None),
    )
    out_specs = (
        P(("dp", "expert"), None),
        P(("dp", "expert"), None),
        P("expert", "dp", None),
        P("expert", "dp", None),
        P("expert", "dp", None),
    )
    return jax.shard_map(
        on_device, mesh=mesh, in_specs=in_specs, out_specs=out_specs, check_vma=False
    )
```

```python
import functools

import jax
import jax.numpy as jnp
from jax import lax
from jax.experimental import pallas as pl
from jax.experimental.pallas import tpu as pltpu
from jax.sharding import PartitionSpec as P

f32 = jnp.float32
bf16 = jnp.bfloat16
highest = lax.Precision.HIGHEST


def dot(lhs, rhs, lhs_dim, rhs_dim, precision=None):
    dims = (((lhs_dim,), (rhs_dim,)), ((), ()))
    return lax.dot_general(lhs, rhs, dims, precision=precision, preferred_element_type=f32)


def plane_exchange(blocks):
    return lax.all_to_all(blocks, "expert", split_axis=0, concat_axis=0, tiled=True)


def core_swap(block):
    size = lax.axis_size("dp")
    return lax.ppermute(block, "dp", [(i, i ^ 1) for i in range(size)])


def z_exchange(blocks):
    size = lax.axis_size("dp")
    groups = [list(range(core, size, 2)) for core in range(2)]
    return lax.all_to_all(
        blocks, "dp", split_axis=0, concat_axis=0, tiled=True, axis_index_groups=groups
    )


def z_reduce_scatter(blocks):
    size = lax.axis_size("dp")
    groups = [list(range(core, size, 2)) for core in range(2)]
    return lax.psum_scatter(
        blocks, "dp", scatter_dimension=0, tiled=True, axis_index_groups=groups
    )


def add(one, other):
    return (one.astype(f32) + other.astype(f32)).astype(bf16)


def pad_blocks(blocks, count):
    return jnp.pad(blocks, ((0, count - blocks.shape[0]),) + ((0, 0),) * (blocks.ndim - 1))


def in_vmem(count):
    return [pl.BlockSpec(memory_space=pltpu.VMEM)] * count


def tables(routed_ref, weight_ref, experts):
    rows = routed_ref.shape[1]
    total = experts * 8
    names = lax.broadcasted_iota(jnp.int32, (experts, rows), 0)
    named = jnp.zeros((experts, rows), f32)
    table = jnp.zeros((experts, rows), f32)
    for k in range(routed_ref.shape[0]):
        hit = routed_ref[k : k + 1, :] == names
        named = jnp.where(hit, 1.0, named)
        table = jnp.where(hit, weight_ref[k : k + 1, :], table)
    counts = jnp.sum(named, axis=1, keepdims=True)
    busy = counts == jnp.max(counts, axis=0, keepdims=True)
    busiest = jnp.max(jnp.where(busy, names, 0)[:, :1], axis=0, keepdims=True)
    cold = jnp.where(busy, 0.0, named)
    first = lax.broadcasted_iota(jnp.int32, (rows, rows), 0)
    second = lax.broadcasted_iota(jnp.int32, (rows, rows), 1)
    before = jnp.where(first < second, 1.0, 0.0)
    rank = dot(cold.astype(bf16), before.astype(bf16), 1, 0)
    code = jnp.where(cold > 0.0, rank + 1.0, 0.0)
    hot_row = jnp.sum(jnp.where(busy, table, 0.0), axis=0, keepdims=True)
    hot_weight = jnp.sum(jnp.where(first == second, hot_row, 0.0), axis=1, keepdims=True)
    owner = lax.broadcasted_iota(jnp.int32, (total, experts), 0) // 8
    spread = owner == lax.broadcasted_iota(jnp.int32, (total, experts), 1)
    spread = jnp.where(spread, 1.0, 0.0)
    code = dot(spread.astype(bf16), code.astype(bf16), 1, 0)
    table = dot(spread, table, 1, 0, highest)
    row = lax.broadcasted_iota(jnp.int32, (total, rows), 0)
    is_token = row % 8 < 4
    place = code == (row % 4 + 1).astype(f32)
    return hot_weight, busiest, place, is_token, jnp.where(place, table, 0.0)


def pack_kernel(
    shard_ref, routed_hbm, weight_hbm, tokens_hbm, cotangent_hbm, gate_hbm, up_hbm, down_hbm, out_ref, hot_ref, busiest_ref,
    tokens_ref, cotangent_ref, weight_ref, routed_ref, gate_ref, up_ref, down_ref, sems, size
):
    moves = []
    sources = (routed_hbm, weight_hbm, tokens_hbm, cotangent_hbm, gate_hbm, up_hbm, down_hbm)
    targets = (routed_ref, weight_ref, tokens_ref, cotangent_ref, gate_ref, up_ref, down_ref)
    for index, (source, target) in enumerate(zip(sources, targets)):
        moves.append(pltpu.make_async_copy(source, target, sems.at[index]))
        moves[index].start()
    rows, features = tokens_ref.shape
    width = gate_ref.shape[1]
    units = width // size
    height, spans = -(-3 * units // 16) * 16, features // 256
    total = out_ref.shape[0]
    experts = total // 8
    moves[0].wait()
    moves[1].wait()
    hot_weight, busiest, place, is_token, spots = tables(routed_ref, weight_ref, experts)
    busiest_ref[...] = jnp.broadcast_to(busiest, busiest_ref.shape)
    moves[2].wait()
    moves[3].wait()
    tokens = tokens_ref[...]
    cotangent = cotangent_ref[...]
    hot_ref[:, :features] = tokens
    hot_ref[:, features:] = (hot_weight * cotangent.astype(f32)).astype(bf16)

    slot_weight = jnp.sum(spots, axis=1, keepdims=True)
    factor = jnp.where(is_token[:, :1], 1.0, slot_weight)
    place = jnp.where(place, 1.0, 0.0)
    picked = dot(jnp.where(is_token, place, 0.0).astype(bf16), tokens, 1, 0)
    picked = picked + dot(jnp.where(is_token, 0.0, place).astype(bf16), cotangent, 1, 0)
    out_ref[:, :features] = (picked * factor).astype(bf16)

    unit = shard_ref[0] * units + lax.broadcasted_iota(jnp.int32, (units, width), 0)
    choose = unit == lax.broadcasted_iota(jnp.int32, (units, width), 1)
    choose = jnp.where(choose, 1.0, 0.0).astype(bf16)
    for move in moves[4:]:
        move.wait()
    pieces = [
        dot(choose, gate_ref[...], 1, 1),
        dot(choose, up_ref[...], 1, 1),
        dot(choose, down_ref[...], 1, 0),
    ]
    if height > 3 * units:
        pieces.append(jnp.zeros((height - 3 * units, features), f32))
    pieces = jnp.concatenate(pieces, axis=0).astype(bf16)
    for span in range(spans):
        out_ref[span * height : span * height + height, features:] = pieces[
            :, span * 256 : span * 256 + 256
        ]
    used = spans * height
    out_ref[used:, features:] = jnp.zeros((total - used, 256), bf16)


def pack(shard, tokens, cotangent, weight, routed, gate, up, down, experts, size):
    rows, features = tokens.shape
    return pl.pallas_call(
        functools.partial(pack_kernel, size=size),
        out_shape=(
            jax.ShapeDtypeStruct((experts * 8, features + 256), bf16),
            jax.ShapeDtypeStruct((rows, 2 * features), bf16),
            jax.ShapeDtypeStruct((8, 128), jnp.int32),
        ),
        in_specs=[pl.BlockSpec(memory_space=pltpu.SMEM)]
        + [pl.BlockSpec(memory_space=pl.ANY)] * 7,
        out_specs=tuple(in_vmem(3)),
        scratch_shapes=[
            pltpu.VMEM((rows, features), bf16),
            pltpu.VMEM((rows, features), bf16),
            pltpu.VMEM(weight.shape, f32),
            pltpu.VMEM(routed.shape, jnp.int32),
            pltpu.VMEM(gate.shape, bf16),
            pltpu.VMEM(up.shape, bf16),
            pltpu.VMEM(down.shape, bf16),
            pltpu.SemaphoreType.DMA((7,)),
        ],
        compiler_params=pltpu.CompilerParams(vmem_limit_bytes=60 * 2**20),
    )(shard, routed, weight, tokens, cotangent, gate, up, down)


def join_kernel(own_kept, own_came, hot_kept, hot_came, joined_ref, pair_ref):
    own_rows = own_kept.shape[1]
    rows = joined_ref.shape[1] - own_rows
    joined_ref[:, :own_rows, :] = add(own_kept[...], own_came[...])
    hot = add(hot_kept[...], hot_came[...])
    joined_ref[:, own_rows:, :] = hot[:, :rows]
    pair_ref[...] = hot[:, rows:]


def join(own_kept, own_came, hot_kept, hot_came, strip):
    depth, own_rows, _ = own_kept.shape
    rows = own_rows + hot_kept.shape[1] - strip
    return pl.pallas_call(
        join_kernel,
        out_shape=(
            jax.ShapeDtypeStruct((depth, rows, 128), bf16),
            jax.ShapeDtypeStruct((depth, strip, 128), bf16),
        ),
        in_specs=in_vmem(4),
        out_specs=tuple(in_vmem(2)),
        compiler_params=pltpu.CompilerParams(vmem_limit_bytes=48 * 2**20),
    )(own_kept, own_came, hot_kept, hot_came)


def pick_kernel(busiest_ref, piece_ref, out_ref):
    out_ref[...] = jnp.broadcast_to(piece_ref[...], out_ref.shape)


def pick(busiest, arrived, features):
    experts = arrived.shape[0]
    shape = (experts, 8, 256)
    grid_spec = pltpu.PrefetchScalarGridSpec(
        num_scalar_prefetch=1,
        grid=(1,),
        in_specs=[pl.BlockSpec((1, 8, 256), lambda i, chosen: (chosen[0], 0, features // 256))],
        out_specs=pl.BlockSpec(shape, lambda i, chosen: (0, 0, 0)),
    )
    return pl.pallas_call(
        pick_kernel, grid_spec=grid_spec, out_shape=jax.ShapeDtypeStruct(shape, bf16)
    )(busiest, arrived)


def total_kernel(parts_ref, out_ref):
    sums = jnp.sum(parts_ref[...].astype(f32), axis=0, keepdims=True).astype(bf16)
    out_ref[...] = jnp.broadcast_to(sums, out_ref.shape)


def total(back):
    shape = (back.shape[0], 8, 256)
    block = back.shape[2] // 256 - 1
    return pl.pallas_call(
        total_kernel,
        grid=(1,),
        in_specs=[pl.BlockSpec(shape, lambda i: (0, 0, block))],
        out_specs=pl.BlockSpec(shape, lambda i: (0, 0, 0)),
        out_shape=jax.ShapeDtypeStruct(shape, bf16),
    )(back)


def own_kernel(
    core_ref, rows_ref, gate_ref, up_ref, down_ref, out_ref, kept_ref, passed_ref, grads, down_grads
):
    features, width = gate_ref.shape
    depth = kept_ref.shape[0]
    half = features // 2
    strip = features // (2 * depth)
    units = width // (2 * depth)
    lanes = width // 128
    core = core_ref[0]
    sides = ((kept_ref, core), (passed_ref, 1 - core))
    rows = rows_ref[:, :features]
    down = down_ref[...]
    gate_value = dot(rows, gate_ref[...], 1, 0)
    up_value = dot(rows, up_ref[...], 1, 0)
    upstream = dot(rows, down, 1, 1)
    count = gate_value.shape[0]
    upstream = pltpu.roll(upstream, count - 4, 0)
    sigmoid = jax.nn.sigmoid(gate_value)
    active = gate_value * sigmoid
    slope = sigmoid * (1.0 + gate_value * (1.0 - sigmoid))
    is_token = lax.broadcasted_iota(jnp.int32, (count, width), 0) % 8 < 4
    hidden = jnp.where(is_token, active * up_value, 0.0)
    shifted = pltpu.roll(hidden, 4, 0).astype(bf16)
    hidden = hidden.astype(bf16)
    gate_delta = jnp.where(is_token, upstream * up_value * slope, 0.0).astype(bf16)
    up_delta = jnp.where(is_token, upstream * active, 0.0).astype(bf16)
    for index, delta in enumerate((gate_delta, up_delta)):
        grads[...] = dot(rows, delta, 0, 0)
        for z in range(depth):
            for ref, side in sides:
                start = pl.multiple_of((2 * z + side) * strip, strip)
                block = grads[pl.ds(start, strip), :].astype(bf16)
                for lane in range(lanes):
                    at = (index * lanes + lane) * strip
                    ref[z, at : at + strip, :] = block[:, lane * 128 : lane * 128 + 128]
    down_grads[...] = dot(shifted, rows, 0, 0)
    base = 2 * lanes * strip
    for z in range(depth):
        for ref, side in sides:
            start = pl.multiple_of((2 * z + side) * units, 8)
            block = down_grads[pl.ds(start, units), :]
            for lane in range(0, features // 128, 2):
                at = base + lane * units
                pair = [block[:, i * 128 : i * 128 + 128] for i in (lane, lane + 1)]
                ref[z, at : at + 2 * units, :] = jnp.concatenate(pair, axis=0).astype(bf16)
    output = dot(hidden, down[:, :half], 1, 0) + dot(shifted, down[:, half:], 1, 0)
    out_ref[...] = output.astype(bf16)


def own_expert(core, rows, gate, up, down, depth):
    features, width = gate.shape
    side = jax.ShapeDtypeStruct((depth, 3 * features * width // (2 * depth) // 128, 128), bf16)
    return pl.pallas_call(
        own_kernel,
        out_shape=(jax.ShapeDtypeStruct((rows.shape[0], features // 2), bf16), side, side),
        in_specs=[pl.BlockSpec(memory_space=pltpu.SMEM)] + in_vmem(4),
        out_specs=tuple(in_vmem(3)),
        scratch_shapes=[pltpu.VMEM((features, width), f32), pltpu.VMEM((width, features), f32)],
        compiler_params=pltpu.CompilerParams(vmem_limit_bytes=48 * 2**20),
    )(core, rows, gate, up, down)


def hot_kernel(
    units, core_ref, rows_ref, blocks_ref, kept_ref, passed_ref, grads_ref, part, pair_part
):
    features = part.shape[1]
    depth = kept_ref.shape[0]
    group = part.shape[0] // (2 * depth)
    spans = features // 256
    height = -(-3 * units // 16) * 16
    core = core_ref[0]
    inputs = rows_ref[:, :features]
    scaled = rows_ref[:, features:]
    sliced = jnp.concatenate(
        [blocks_ref[span * height : span * height + height, :] for span in range(spans)], axis=1
    )
    down = sliced[2 * units :]
    both = dot(sliced[: 2 * units], inputs, 1, 1)
    upstream = dot(down, scaled, 1, 1)[:units]
    gate_value, up_value = both[:units], both[units:]
    sigmoid = jax.nn.sigmoid(gate_value)
    active = gate_value * sigmoid
    slope = sigmoid * (1.0 + gate_value * (1.0 - sigmoid))
    pair = jnp.concatenate([upstream * up_value * slope, upstream * active], axis=0)
    spare = jnp.zeros((height - 3 * units, gate_value.shape[1]), f32)
    hidden = active * up_value
    if spare.shape[0]:
        hidden = jnp.concatenate([hidden, spare], axis=0)
    hidden = hidden.astype(bf16)
    part[...] = dot(hidden, down, 0, 0)
    empty = jnp.zeros_like(pair)
    spread = [jnp.where(core == 0, pair, empty), jnp.where(core == 1, pair, empty)]
    if 4 * units < 128:
        spread.append(jnp.zeros((128 - 4 * units, pair.shape[1]), f32))
    spread = jnp.concatenate(spread, axis=0).astype(bf16)
    pair_part[...] = dot(inputs, spread, 0, 1)
    strip = features // (2 * depth)
    wide = group * (features // 128)
    for z in range(depth):
        for ref, side in ((kept_ref, core), (passed_ref, 1 - core)):
            start = pl.multiple_of((2 * z + side) * group, group)
            block = part[pl.ds(start, group), :].astype(bf16)
            for lane in range(features // 128):
                ref[z, lane * group : lane * group + group, :] = block[
                    :, lane * 128 : lane * 128 + 128
                ]
            start = pl.multiple_of((2 * z + side) * strip, strip)
            ref[z, wide:, :] = pair_part[pl.ds(start, strip), :].astype(bf16)
    grads = dot(hidden, scaled, 1, 0)[:units]
    for lane in range(0, features // 128, 2):
        both = [grads[:, i * 128 : i * 128 + 128] for i in (lane, lane + 1)]
        grads_ref[lane * units : (lane + 2) * units, :] = jnp.concatenate(both, 0).astype(bf16)
    used = features // 128 * units
    grads_ref[used:, :] = jnp.zeros((grads_ref.shape[0] - used, 128), bf16)


def hot_expert(core, gathered, blocks, units, depth):
    total, features = gathered.shape[0], gathered.shape[1] // 2
    height = total // (2 * depth) * features // 128 + features // (2 * depth)
    side = jax.ShapeDtypeStruct((depth, height, 128), bf16)
    return pl.pallas_call(
        functools.partial(hot_kernel, units),
        out_shape=(side, side, jax.ShapeDtypeStruct((blocks.shape[0], 128), bf16)),
        in_specs=[pl.BlockSpec(memory_space=pltpu.SMEM)] + in_vmem(2),
        out_specs=tuple(in_vmem(3)),
        scratch_shapes=[
            pltpu.VMEM((total, features), f32),
            pltpu.VMEM((features, 128), f32),
        ],
        compiler_params=pltpu.CompilerParams(vmem_limit_bytes=48 * 2**20),
    )(core, gathered, blocks)


def middle_kernel(
    units, routed_ref, weight_ref, cotangent_ref, back_ref, summed_ref,
    layer_ref, route_ref, gate_ref, up_ref, down_ref, spread_ref
):
    rows, features = cotangent_ref.shape
    half = features // 2
    strip, width = gate_ref.shape
    experts = back_ref.shape[0] // 8
    hot_weight, busiest, place, is_token, spots = tables(routed_ref, weight_ref, experts)
    cotangent = cotangent_ref[...]
    results = back_ref[:, :half]
    own_rows = summed_ref.shape[0] - rows * (features // 128)
    blocks = [
        summed_ref[own_rows + i * rows : own_rows + (i + 1) * rows, :]
        for i in range(features // 128)
    ]
    hot_out = jnp.concatenate(blocks, axis=1).astype(f32)
    sides = []
    for side in (jnp.where(is_token, spots, 0.0), jnp.where(is_token, 0.0, spots)):
        high = side.astype(bf16)
        low = (side - high.astype(f32)).astype(bf16)
        sides.append(dot(high, results, 0, 0) + dot(low, results, 0, 0))
    layer = jnp.concatenate(sides, axis=1) + hot_weight * hot_out
    layer_ref[...] = layer.astype(bf16)

    left = dot(results, cotangent[:, :half], 1, 1)
    right = dot(results, cotangent[:, half:], 1, 1)
    products = jnp.where(place, jnp.where(is_token, left, right), 0.0)
    hot_column = jnp.sum(hot_out * cotangent.astype(f32), axis=1, keepdims=True)
    first = lax.broadcasted_iota(jnp.int32, (rows, rows), 0)
    second = lax.broadcasted_iota(jnp.int32, (rows, rows), 1)
    hot_row = jnp.sum(jnp.where(first == second, hot_column, 0.0), axis=0, keepdims=True)
    owner = lax.broadcasted_iota(jnp.int32, products.shape, 0) // 8
    for k in range(routed_ref.shape[0]):
        named = routed_ref[k : k + 1, :]
        cold = jnp.sum(jnp.where(owner == named, products, 0.0), axis=0, keepdims=True)
        route_ref[k : k + 1, :] = cold + jnp.where(named == busiest, hot_row, 0.0)

    lanes = width // 128
    for index, ref in enumerate((gate_ref, up_ref)):
        for lane in range(lanes):
            at = (index * lanes + lane) * strip
            ref[:, lane * 128 : lane * 128 + 128] = summed_ref[at : at + strip, :].astype(f32)
    base = 2 * lanes * strip
    unpair(down_ref, summed_ref, base, 0, units)

    shape = (spread_ref.shape[0], 2 * width)
    lane = lax.broadcasted_iota(jnp.int32, (shape[0], 1), 0)
    within = lane % 128
    column = (within % (2 * units)) // units * width + within % units
    column = column + (lane // 128 * 2 + within // (2 * units)) * units
    column = jnp.where(within < 4 * units, column, -1)
    match = lax.broadcasted_iota(jnp.int32, shape, 1) == column
    spread_ref[...] = jnp.where(match, 1.0, 0.0).astype(bf16)


def unpair(out_ref, from_ref, base, lane_base, units):
    for lane in range(0, out_ref.shape[1] // 128, 2):
        at = base + lane * units
        pair = from_ref[at : at + 2 * units, lane_base : lane_base + 128].astype(f32)
        out_ref[:, lane * 128 : lane * 128 + 128] = pair[:units]
        out_ref[:, lane * 128 + 128 : lane * 128 + 256] = pair[units:]


def middle(routed, weight, cotangent, back, summed, units, strip, depth):
    rows, features = cotangent.shape
    width = units * 2 * depth
    return pl.pallas_call(
        functools.partial(middle_kernel, units),
        out_shape=(
            jax.ShapeDtypeStruct((rows, features), bf16),
            jax.ShapeDtypeStruct(weight.shape, f32),
            jax.ShapeDtypeStruct((strip, width), f32),
            jax.ShapeDtypeStruct((strip, width), f32),
            jax.ShapeDtypeStruct((units, features), f32),
            jax.ShapeDtypeStruct((depth * 128, 2 * width), bf16),
        ),
        in_specs=in_vmem(5),
        out_specs=tuple(in_vmem(6)),
        compiler_params=pltpu.CompilerParams(vmem_limit_bytes=48 * 2**20),
    )(routed, weight, cotangent, back, summed)


def last_kernel(
    units, home_ref, blocks_ref, gate_ref, up_ref, down_ref, spread_ref,
    gate_out, up_out, down_out, scratch
):
    strip, width = gate_ref.shape
    depth = spread_ref.shape[0] // 128
    home = home_ref[0] == 1
    blocks = [blocks_ref[z * strip : (z + 1) * strip, :128] for z in range(depth)]
    pair = dot(jnp.concatenate(blocks, axis=1), spread_ref[...], 1, 0)
    gate_out[...] = gate_ref[...] + jnp.where(home, pair[:, :width], 0.0)
    up_out[...] = up_ref[...] + jnp.where(home, pair[:, width:], 0.0)
    unpair(scratch, blocks_ref, 0, 128, units)
    down_out[...] = down_ref[...] + jnp.where(home, scratch[...], 0.0)


def last(home, blocks, gate, up, down, spread):
    units = down.shape[0]
    return pl.pallas_call(
        functools.partial(last_kernel, units),
        out_shape=tuple(jax.ShapeDtypeStruct(x.shape, f32) for x in (gate, up, down)),
        in_specs=[pl.BlockSpec(memory_space=pltpu.SMEM)] + in_vmem(5),
        out_specs=tuple(in_vmem(3)),
        scratch_shapes=[pltpu.VMEM(down.shape, f32)],
        compiler_params=pltpu.CompilerParams(vmem_limit_bytes=48 * 2**20),
    )(home, blocks, gate, up, down, spread)


def on_device(
    tokens, cotangent, route_weight, routed_experts, gate_weights, up_weights, down_weights
):
    experts = lax.axis_size("expert")
    size = lax.axis_size("dp")
    depth = size // 2
    mine = lax.axis_index("expert")
    shard = lax.axis_index("dp")
    core = shard % 2
    core_word = core.astype(jnp.int32).reshape(1)
    rows, features = tokens.shape
    half = features // 2
    gate, up, down = gate_weights[0], up_weights[0], down_weights[0]
    width = gate.shape[1]
    units = width // size
    strip = features // size

    shard_word = shard.astype(jnp.int32).reshape(1)
    outgoing, hot_rows, found = pack(
        shard_word,
        tokens,
        cotangent,
        route_weight.T,
        routed_experts.T,
        gate,
        up,
        down,
        experts,
        size,
    )
    gathered = lax.all_gather(hot_rows, "dp", axis=0, tiled=True)
    arrived = plane_exchange(outgoing.reshape(experts, 8, features + 256))
    picked = pick(found[0, :1], arrived, features)
    arrived, picked, routed, weight = lax.optimization_barrier(
        (arrived, picked, routed_experts.T, route_weight.T)
    )
    blocks = plane_exchange(picked)
    returning, own_kept, own_passed = own_expert(
        core_word, arrived.reshape(experts * 8, features + 256), gate, up, down, depth
    )
    blocks, own_passed = lax.optimization_barrier((blocks, own_passed))
    own_came = core_swap(own_passed)
    hot_kept, hot_passed, hot_grads = hot_expert(
        core_word, gathered, blocks.reshape(experts * 8, 256), units, depth
    )
    hot_came = core_swap(hot_passed)
    joined, pair = join(own_kept, own_came, hot_kept, hot_came, strip)
    summed = z_reduce_scatter(joined)[0]
    pair = pad_blocks(z_exchange(pair).reshape(depth * strip // 8, 8, 128), experts)

    back = plane_exchange(
        jnp.concatenate(
            [returning.reshape(experts, 8, half), pair, hot_grads.reshape(experts, 8, 128)], axis=2
        )
    )
    hot_blocks = plane_exchange(total(back))
    layer_out, route_gradient, own_gate, own_up, own_down, spread = middle(
        routed, weight, cotangent, back.reshape(experts * 8, -1), summed, units, strip, depth
    )
    home = (mine == found[0, 0]).astype(jnp.int32).reshape(1)
    gate_gradient, up_gradient, down_gradient = last(
        home, hot_blocks.reshape(experts * 8, 256), own_gate, own_up, own_down, spread
    )
    return (
        layer_out,
        route_gradient.T,
        gate_gradient[None],
        up_gradient[None],
        down_gradient[None],
    )


def solution(mesh):
    in_specs = (
        P(("dp", "expert"), None),
        P(("dp", "expert"), None),
        P(("dp", "expert"), None),
        P(("dp", "expert"), None),
        P("expert", None, None),
        P("expert", None, None),
        P("expert", None, None),
    )
    out_specs = (
        P(("dp", "expert"), None),
        P(("dp", "expert"), None),
        P("expert", "dp", None),
        P("expert", "dp", None),
        P("expert", "dp", None),
    )
    return jax.shard_map(
        on_device, mesh=mesh, in_specs=in_specs, out_specs=out_specs, check_vma=False
    )
```
